128 devices in a mesh: pipe: 16 (over y, x), mp: 8 (over z, core).
Axes of the slice: x: 4, y: 4, z: 4, core: 2. Of those that a mesh axis runs over, the one named last changes fastest.
Arguments:
- context: bfloat16 [512, 4096], P('pipe', 'mp'), may hold values from -6 to 6
- residual_in: bfloat16 [512, 4608], P('pipe', 'mp'), may hold values from -6 to 6
- o_weight: bfloat16 [4096, 4608], P('mp', 'pipe'), may hold values from -0.09375 to 0.09375
- post_gain: float32 [4608], replicated, may hold values from 0.1 to 1.9
- final_gain: float32 [4608], replicated, may hold values from 0.1 to 1.9
- head_weight: bfloat16 [4608, 131072], P(None, ('pipe', 'mp')), may hold values from -0.26516504 to 0.26516504
- targets: int32 [512], replicated, may hold values from 0 to 131071
Outputs:
- mean_loss: float32 [], replicated
- head_grad: bfloat16 [4608, 131072], P(None, ('pipe', 'mp'))
- o_grad: bfloat16 [4096, 4608], P('mp', 'pipe')
- d_residual: bfloat16 [512, 4608], P('pipe', 'mp')
- d_context: bfloat16 [512, 4096], P('pipe', 'mp')
The draws below stay inside these ranges and needn't reach their ends.
All inputs are finite; a program needn't handle non-finite values.
Results may differ from the reference program's by a relative error of at most 0.006.
Values may be sent and summed in bfloat16 or wider, within the bound.
A program may use at most 128 MiB of HBM per device.

```python
import math
import jax
import jax.numpy as jnp
from jax import lax

D = 4608
HD = 4096
TOKENS = 512
VOCAB = 131072


def draw_head_weight(key, part):
    key = jax.random.fold_in(key, 7)
    base_key, scale_key = jax.random.split(key)
    base = jnp.clip(jax.random.normal(base_key, (D, VOCAB), jnp.float32), -4.0, 4.0)
    column_scale = jnp.exp(jax.random.uniform(scale_key, (VOCAB,), jnp.float32, math.log(0.4), math.log(4.0)))
    tilt = jnp.exp(math.log(1.12) * jnp.arange(VOCAB, dtype=jnp.float32) / max(VOCAB - 1, 1))
    return (base * (column_scale * tilt)[None, :] / math.sqrt(D)).astype(jnp.bfloat16)


def touch_ends(values, stream_key, smallest, high):
    longest = values.shape.index(max(values.shape))
    spots = []
    for shift in (0, 1):
        where = [jax.random.randint(jax.random.fold_in(stream_key, axis), (), 0, length) for axis, length in enumerate(values.shape)]
        where[longest] = (where[longest] + shift) % values.shape[longest]
        spots.append(tuple(where))
    return values.at[spots[0]].set(smallest).at[spots[1]].set(high)


def block_scale(stream_key, shape, cuts, least, high):
    factor_of, own = 1.0, jax.random.fold_in(stream_key, 6)
    for axis_at, blocks in cuts:
        steps = jnp.exp(jax.random.uniform(jax.random.fold_in(own, axis_at), (blocks,), jnp.float32, least / len(cuts), high / len(cuts)))
        factor_of = factor_of * jnp.repeat(steps, shape[axis_at] // blocks).reshape([-1 if axis == axis_at else 1 for axis in range(len(shape))])
    return factor_of


def gaussian(key, extent, deviation, limit, pieces=(), held_as=jnp.bfloat16):
    array = jax.random.normal(key, extent, jnp.float32) * deviation
    if len(pieces) > 0:
        array = block_scale(key, extent, pieces, -0.22, 0.18) * array
    return jnp.clip(array, min=-limit, max=limit).astype(held_as)


def setup_inputs(seed: int = 0) -> dict:
    splits = jax.random.split(jax.random.key(seed), 8)
    return {
        "context": gaussian(splits[0], (TOKENS, HD), 1.0, 6.0, ((0, 16), (1, 8))),
        "residual_in": gaussian(splits[1], (TOKENS, D), 1.0, 6.0, ((0, 16), (1, 8))),
        "o_weight": gaussian(splits[2], (HD, D), HD ** -0.5, 0.09375, ((0, 8), (1, 16))),
        "post_gain": jnp.clip(1.0 + 0.18 * jax.random.normal(splits[3], (D,), jnp.float32), 0.1, 1.9),
        "final_gain": jnp.clip(1.0 + 0.18 * jax.random.normal(splits[4], (D,), jnp.float32), 0.1, 1.9),
        "head_weight": draw_head_weight(jax.random.fold_in(splits[7], 71), 0),
        "targets": touch_ends(jax.random.randint(splits[6], (TOKENS,), 0, VOCAB), jax.random.fold_in(splits[6], 1), 0, VOCAB - 1).astype(jnp.int32),
    }


epsilon = 1e-06
softcap = 30.0

def inverse_rms(values):
    return lax.rsqrt(lax.optimization_barrier(jnp.mean(values * values, axis=-1, keepdims=True)) + epsilon)

def reference(context, residual_in, o_weight, post_gain, final_gain, head_weight, targets):
    attn_full = jnp.dot(context, o_weight, preferred_element_type=jnp.float32)
    inv_attn = inverse_rms(attn_full)
    stream = residual_in.astype(jnp.float32) + attn_full * inv_attn * post_gain
    inv_stream = inverse_rms(stream)
    normed = (stream * inv_stream * final_gain).astype(jnp.bfloat16)
    logits = jnp.dot(normed, head_weight, preferred_element_type=jnp.float32)
    capped = softcap * jnp.tanh(logits / softcap)
    exp_logits = jnp.exp(capped)
    columns = lax.iota(jnp.int32, VOCAB)
    target_hits = columns[None, :] == targets[:, None]
    totals = lax.optimization_barrier(jnp.sum(exp_logits, axis=-1))
    target_logit = lax.optimization_barrier(jnp.sum(jnp.where(target_hits, capped, jnp.float32(0.0)), axis=-1))
    mean_loss = jnp.mean(jnp.log(totals) - target_logit)
    logit_grad = (exp_logits / totals[:, None] - target_hits.astype(jnp.float32)) * (1.0 - (capped / softcap) ** 2)
    logit_grad = logit_grad.astype(jnp.bfloat16)
    head_grad = jnp.dot(normed.T, logit_grad, preferred_element_type=jnp.float32).astype(jnp.bfloat16)
    grad_normed = jnp.dot(logit_grad, head_weight.T, preferred_element_type=jnp.float32)
    upstream_grad = grad_normed * final_gain
    grad_stream = inv_stream * (upstream_grad - stream * inv_stream ** 2 * lax.optimization_barrier(jnp.mean(stream * upstream_grad, axis=-1, keepdims=True)))
    scaled_grad = grad_stream * post_gain
    grad_attn = inv_attn * (scaled_grad - attn_full * inv_attn ** 2 * lax.optimization_barrier(jnp.mean(attn_full * scaled_grad, axis=-1, keepdims=True)))
    grad_attn = grad_attn.astype(jnp.bfloat16)
    d_residual = grad_stream.astype(jnp.bfloat16)
    d_context = jnp.dot(grad_attn, o_weight.T, preferred_element_type=jnp.float32).astype(jnp.bfloat16)
    o_grad = jnp.dot(context.T, grad_attn, preferred_element_type=jnp.float32).astype(jnp.bfloat16)
    return (mean_loss, head_grad, o_grad, d_residual, d_context)
```

```python
import jax
import jax.numpy as jnp
from jax import lax
from jax.experimental import pallas as pl
from jax.experimental.pallas import tpu as pltpu
from jax.sharding import PartitionSpec as P

epsilon = 1e-06
softcap = 30.0
MESH = pl.DeviceIdType.MESH
F32, BF16 = jnp.float32, jnp.bfloat16

WIDTH = 4608
SHARE = 1152
PANELS = 9
COLS = 288
GATHER = (("z", "x", "y"), ("x", "y", "z"), ("y", "z", "x"))
NEAR = (1, 3, 2)


def remote(src, dst, send, recv, device):
    return pltpu.make_async_remote_copy(
        src_ref=src, dst_ref=dst, send_sem=send, recv_sem=recv, device_id=device, device_id_type=MESH
    )


def place(at):
    return (at["y"] * 4 + at["x"], at["z"] * 2 + at["c"])


def moved(at, dim, by):
    size = 2 if dim == "c" else 4
    return {**at, dim: lax.rem(at[dim] + by, size)}


def lanes(start, size):
    return pl.ds(pl.multiple_of(start, 128), size)


def rows_of(start, size):
    return pl.ds(pl.multiple_of(start, 16), size)


def section(
    ctx_ref, res_ref, ow_ref, pg_ref, fg_ref, w_hbm, tgt_ref,
    n_out, g_out, loss_out, og_out, dres_out, dctx_out,
    wv, ctx, ow, rres, aout, ain, attn_s, stream_s, nbuf, gath, cap, tgt, hot, part, psrc, pipe_in, mp_in, scale, grad,
    keep, sib_out, sib_in, first, r1a, r1b, r1c, s2, own2, r2a, r2b, r2c, s3, r3,
    gsum, cbuf, gout, gin, dcs, dcr, ogs, ogr, dsend, drecv,
    w_sem, ctx_ss, ctx_rs, sib_ss, sib_rs, at_ss, at_rs, z_ss, z_rs, ag_ss, ag_rs, agc_ss, agc_rs, tp_ss, tp_rs, tm_ss, tm_rs,
    rc_ss, rc_rs, rs_ss, rs_rs, ga_ss, ga_rs, dc_ss, dc_rs, out_sem,
):
    p, m = lax.axis_index("pipe"), lax.axis_index("mp")
    y, x, z, c = p // 4, p % 4, m // 2, m % 2
    at = {"y": y, "x": x, "z": z, "c": c}
    sib = (p, z * 2 + (1 - c))
    me = p * 2 + c
    peer32 = lambda j: lax.rem(me + j, 32)
    place32 = lambda i: (i // 2, z * 2 + i % 2)

    w_copies = [
        pltpu.make_async_copy(w_hbm.at[i], wv.at[:, pl.ds(i * 128, 128), :], w_sem.at[i]) for i in range(4)
    ]
    for copy in w_copies:
        copy.start()

    barrier = pltpu.get_barrier_semaphore()

    def greet(device):
        pl.semaphore_signal(barrier, inc=1, device_id=device, device_id_type=MESH)

    def greet32(j, _):
        greet(place32(peer32(j)))
        return 0

    lax.fori_loop(1, 32, greet32, 0)
    for by in (1, 2, 3):
        zz = lax.rem(z + by, 4)
        for cc in (0, 1):
            greet((p, zz * 2 + cc))
        for xx in range(4):
            greet((z * 4 + xx, zz * 2 + c))

    @pl.when(y != z)
    def _():
        def greet16(i, _):
            greet((i, y * 2 + c))
            return 0

        lax.fori_loop(0, 16, greet16, 0)

    pl.semaphore_wait(barrier, 49 + 16 * jnp.where(y != z, 1, 0))

    my_lanes = lanes(c * 512, 512)

    def ctx_send(j, _):
        i = peer32(j)
        remote(
            ctx_ref.at[rows_of((i % 2) * 16, 16)], ctx.at[p, :, my_lanes], ctx_ss.at[j], ctx_rs.at[j], place32(i)
        ).start()
        return 0

    lax.fori_loop(1, 32, ctx_send, 0)
    half = rows_of(c * 512, 512)
    ow_copy = remote(ow_ref, ow.at[half], sib_ss.at[0], sib_rs.at[0], sib)
    ow_copy.start()
    res_copy = remote(res_ref.at[rows_of((1 - c) * 16, 16)], rres, sib_ss.at[1], sib_rs.at[1], sib)
    res_copy.start()
    ctx[p, :, my_lanes] = ctx_ref[rows_of(c * 16, 16), :]
    ow[half, :] = ow_ref[...]
    for i in range(4):
        block = jnp.broadcast_to(tgt_ref[i : i + 1, :], (128, 128)).T
        for j in range(4):
            for cc in range(2):
                tgt[cc * 256 + (i * 4 + j) * 16 : cc * 256 + (i * 4 + j + 1) * 16, :] = block[
                    j * 32 + cc * 16 : j * 32 + (cc + 1) * 16, :
                ]

    def ctx_wait(j, _):
        i = lax.rem(me + 32 - j, 32)
        dst = ctx.at[i // 2, :, lanes((i % 2) * 512, 512)]
        remote(dst, dst, ctx_ss.at[j], ctx_rs.at[j], place32(i)).wait_recv()
        return 0

    lax.fori_loop(1, 32, ctx_wait, 0)
    remote(ow.at[rows_of((1 - c) * 512, 512)], ow.at[rows_of((1 - c) * 512, 512)], sib_ss.at[0], sib_rs.at[0], sib).wait_recv()

    aout[...] = jnp.dot(
        ctx[...].reshape(256, 1024), ow[...], preferred_element_type=F32
    ).reshape(16, 16, COLS)

    def attn_send(i, _):
        home = jnp.logical_and(i == p, y == z)

        @pl.when(jnp.logical_not(home))
        def _():
            remote(aout.at[i], ain.at[x, z], at_ss.at[i], at_rs.at[x, z], (i, y * 2 + c)).start()

        @pl.when(home)
        def _():
            ain[x, z] = aout[i]

        return 0

    lax.fori_loop(0, 16, attn_send, 0)
    res_copy.wait_recv()

    def attn_wait(i, _):
        xx, zz = i // 4, i % 4
        home = jnp.logical_and(jnp.logical_and(xx == x, zz == z), y == z)

        @pl.when(jnp.logical_not(home))
        def _():
            remote(ain.at[xx, zz], ain.at[xx, zz], at_ss.at[0], at_rs.at[xx, zz], (z * 4 + xx, zz * 2 + c)).wait_recv()

        return 0

    lax.fori_loop(0, 16, attn_wait, 0)
    attn = jnp.concatenate([ain[i, 0] + ain[i, 1] + ain[i, 2] + ain[i, 3] for i in range(4)], axis=1)
    mine, other = res_ref[rows_of(c * 16, 16), :].astype(F32), rres[...].astype(F32)
    residual = jnp.where(c == 0, jnp.concatenate([mine, other], axis=1), jnp.concatenate([other, mine], axis=1))
    share = lanes(z * SHARE, SHARE)
    post, final = pg_ref[:, share], fg_ref[:, share]

    def z_sum(which, value):
        nbuf[which, z] = value
        for by in NEAR:
            remote(
                nbuf.at[which, z], nbuf.at[which, z], z_ss.at[which, by - 1], z_rs.at[which, by - 1],
                place(moved(at, "z", by)),
            ).start()
        for by in NEAR:
            src = nbuf.at[which, lax.rem(z + 4 - by, 4)]
            remote(src, src, z_ss.at[which, by - 1], z_rs.at[which, by - 1], place(moved(at, "z", 4 - by))).wait_recv()
        return nbuf[which, 0] + nbuf[which, 1] + nbuf[which, 2] + nbuf[which, 3]

    def row_sum(value):
        return jnp.broadcast_to(jnp.sum(value, axis=1, keepdims=True), (16, 128))

    attn_sq = z_sum(0, row_sum(attn * attn))[:, :1]
    inv_attn = lax.rsqrt(attn_sq / WIDTH + epsilon)
    stream = residual + attn * inv_attn * post
    stream_sq = z_sum(1, row_sum(stream * stream))[:, :1]
    inv_stream = lax.rsqrt(stream_sq / WIDTH + epsilon)
    normed = (stream * inv_stream * final).astype(BF16)
    attn_s[...] = attn
    stream_s[...] = stream
    nbuf[4, 0] = jnp.broadcast_to(inv_attn, (16, 128))
    nbuf[4, 1] = jnp.broadcast_to(inv_stream, (16, 128))

    my_z = lanes(z * 128, 128)
    for q in range(PANELS):
        gath[q, c, y, x, :, my_z] = normed[:, q * 128 : (q + 1) * 128]

    def region(q, here, done):
        return gath.at[
            q,
            here["c"],
            pl.ds(0, 4) if "y" in done else here["y"],
            pl.ds(0, 4) if "x" in done else here["x"],
            :,
            pl.ds(0, 512) if "z" in done else lanes(here["z"] * 128, 128),
        ]

    def ag_start(q, stage):
        dims = GATHER[q % 3]
        src = region(q, at, dims[:stage])
        for by in NEAR:
            remote(
                src, src, ag_ss.at[q, stage, by - 1], ag_rs.at[q, stage, by - 1], place(moved(at, dims[stage], by))
            ).start()

    def ag_wait(q, stage):
        dims = GATHER[q % 3]
        for by in NEAR:
            source = moved(at, dims[stage], 4 - by)
            src = region(q, source, dims[:stage])
            remote(src, src, ag_ss.at[q, stage, by - 1], ag_rs.at[q, stage, by - 1], place(source)).wait_recv()

    for q in range(PANELS):
        ag_start(q, 0)
    for stage in (1, 2):
        for q in range(PANELS):
            ag_wait(q, stage - 1)
            ag_start(q, stage)
    for copy in w_copies:
        copy.wait()

    def logits(third, which):
        rows = lambda: rows_of(which * 256, 256)

        @pl.loop(0, 4)
        def _(block):
            cols = lanes(block * 256, 256)
            total = None
            for q in range(third * 3, third * 3 + 3):
                term = jnp.dot(gath[q, which].reshape(256, 512), wv[q, :, cols], preferred_element_type=F32)
                total = term if total is None else total + term
            if third > 0:
                total = total + cap[rows(), cols]
            if third < 2:
                cap[rows(), cols] = total
            else:
                capped = softcap * jnp.tanh(total * (1.0 / softcap))
                cap[rows(), cols] = capped
                expd = jnp.exp(capped)
                first_col = m * 1024 + p * 8192 + block * 256
                ids = lax.broadcasted_iota(jnp.int32, (256, 128), 1) + first_col
                wanted = tgt[rows(), :]
                sums = expd[:, :128] + expd[:, 128:]
                hits = jnp.where(ids == wanted, capped[:, :128], 0.0) + jnp.where(
                    ids + 128 == wanted, capped[:, 128:], 0.0
                )

                @pl.when(block == 0)
                def _():
                    part[rows(), :] = sums
                    hot[rows(), :] = hits

                @pl.when(block > 0)
                def _():
                    part[rows(), :] += sums
                    hot[rows(), :] += hits

    for third in range(3):
        for q in range(third * 3, third * 3 + 3):
            ag_wait(q, 2)
            remote(gath.at[q, c], gath.at[q, c], agc_ss.at[q], agc_rs.at[q], sib).start()
        logits(third, c)
        for q in range(third * 3, third * 3 + 3):
            remote(gath.at[q, 1 - c], gath.at[q, 1 - c], agc_ss.at[q], agc_rs.at[q], sib).wait_recv()
        logits(third, 1 - c)
    n_copy = pltpu.make_async_copy(gath, n_out, out_sem.at[0])
    n_copy.start()

    for i in range(4):
        psrc[i : i + 1, :] = jnp.sum(part[i * 128 : (i + 1) * 128, :].T, axis=0, keepdims=True)
        psrc[i + 4 : i + 5, :] = jnp.sum(hot[i * 128 : (i + 1) * 128, :].T, axis=0, keepdims=True)
    pipe_in[p] = psrc[...]

    def pipe_send(j, _):
        remote(psrc, pipe_in.at[p], tp_ss.at[j], tp_rs.at[j], (lax.rem(p + j, 16), m)).start()
        return 0

    def pipe_wait(j, _):
        i = lax.rem(p + 16 - j, 16)
        remote(psrc, pipe_in.at[i], tp_ss.at[j], tp_rs.at[j], (i, m)).wait_recv()
        return 0

    lax.fori_loop(1, 16, pipe_send, 0)
    lax.fori_loop(1, 16, pipe_wait, 0)
    mp_in[m] = jnp.sum(pipe_in[...], axis=0)

    def mp_send(j, _):
        remote(mp_in.at[m], mp_in.at[m], tm_ss.at[j], tm_rs.at[j], (p, lax.rem(m + j, 8))).start()
        return 0

    def mp_wait(j, _):
        i = lax.rem(m + 8 - j, 8)
        remote(mp_in.at[i], mp_in.at[i], tm_ss.at[j], tm_rs.at[j], (p, i)).wait_recv()
        return 0

    lax.fori_loop(1, 8, mp_send, 0)
    lax.fori_loop(1, 8, mp_wait, 0)
    sums = jnp.sum(mp_in[...], axis=0)
    totals, target_logit = sums[:4], sums[4:]
    loss_out[...] = jnp.sum(
        jnp.sum(jnp.log(totals) - target_logit, axis=0, keepdims=True), axis=1, keepdims=True
    ) * (1.0 / 512)
    inverse = 1.0 / totals
    for i in range(4):
        scale[i * 128 : (i + 1) * 128, :] = jnp.broadcast_to(inverse[i : i + 1, :], (128, 128)).T

    @pl.loop(0, 16)
    def _(block):
        rows = rows_of(block * 32, 32)
        wanted, inv = tgt[rows, :], scale[rows, :]
        ids = lax.broadcasted_iota(jnp.int32, (32, 128), 1) + (m * 1024 + p * 8192)
        for j in range(8):
            cols = slice(j * 128, (j + 1) * 128)
            capped = cap[rows, cols]
            ratio = capped * (1.0 / softcap)
            hit = jnp.where(ids + j * 128 == wanted, 1.0, 0.0)
            grad[rows, cols] = ((jnp.exp(capped) * inv - hit) * (1.0 - ratio * ratio)).astype(BF16)

    g_copy = pltpu.make_async_copy(grad, g_out, out_sem.at[1])
    g_copy.start()

    def grad_dot(q, which):
        rows = rows_of(which * 256, 256)
        return lax.dot_general(grad[rows, :], wv[q], (((1,), (1,)), ((), ())), preferred_element_type=F32).reshape(
            4, 4, 16, 512
        )

    def rs_sib(q):
        sib_out[q] = grad_dot(q, 1 - c).astype(BF16)
        remote(sib_out.at[q], sib_in.at[q], rc_ss.at[q], rc_rs.at[q], sib).start()

    def piece(ref, dim, index, left, lead):
        where = list(lead)
        for d in ("y", "x"):
            if d in left:
                where.append(index if d == dim else pl.ds(0, 4))
        where.append(pl.ds(0, 16))
        if "z" in left:
            where.append(lanes(index * 128, 128) if dim == "z" else pl.ds(0, 512))
        else:
            where.append(pl.ds(0, 128))
        return tuple(where)

    r1 = (r1a, r1b, r1c)
    r2 = (r2a, r2b, r2c)
    dims_of = lambda q: GATHER[q % 3][::-1]

    def rs_first(q):
        remote(sib_out.at[q], sib_in.at[q], rc_ss.at[q], rc_rs.at[q], sib).wait_recv()
        total = keep[q] + sib_in[q].astype(F32)
        keep[q] = total
        first[q] = total.astype(BF16)
        dim = dims_of(q)[0]
        for by in NEAR:
            there = moved(at, dim, by)
            src = first.at[piece(first, dim, there[dim], ("y", "x", "z"), (q,))]
            remote(src, r1[q % 3].at[q // 3, by - 1], rs_ss.at[q, 0, by - 1], rs_rs.at[q, 0, by - 1], place(there)).start()

    def rs_recv(q, stage, ref):
        dim = dims_of(q)[stage]
        for by in NEAR:
            dst = ref.at[by - 1]
            remote(
                dst, dst, rs_ss.at[q, stage, by - 1], rs_rs.at[q, stage, by - 1], place(moved(at, dim, 4 - by))
            ).wait_recv()

    def rs_second(q):
        k, r = q % 3, q // 3
        got = r1[k].at[r]
        rs_recv(q, 0, got)
        dims = dims_of(q)
        left = [d for d in ("y", "x", "z") if d != dims[0]]
        total = keep[piece(keep, dims[0], at[dims[0]], ("y", "x", "z"), (q,))]
        total = total + got[0].astype(F32) + got[1].astype(F32) + got[2].astype(F32)
        own2[k][r] = total
        s2[k][r] = total.astype(BF16)
        for by in NEAR:
            there = moved(at, dims[1], by)
            src = s2[k].at[piece(s2[k], dims[1], there[dims[1]], left, (r,))]
            remote(src, r2[k].at[r, by - 1], rs_ss.at[q, 1, by - 1], rs_rs.at[q, 1, by - 1], place(there)).start()

    def rs_third(q):
        k, r = q % 3, q // 3
        got = r2[k].at[r]
        rs_recv(q, 1, got)
        dims = dims_of(q)
        left = [d for d in ("y", "x", "z") if d != dims[0]]
        total = own2[k][piece(own2[k], dims[1], at[dims[1]], left, (r,))]
        total = total + got[0].astype(F32) + got[1].astype(F32) + got[2].astype(F32)
        s3[k][r] = total
        for by in NEAR:
            there = moved(at, dims[2], by)
            src = s3[k].at[piece(s3[k], dims[2], there[dims[2]], [dims[2]], (r,))]
            remote(src, r3.at[q, by - 1], rs_ss.at[q, 2, by - 1], rs_rs.at[q, 2, by - 1], place(there)).start()

    def rs_last(q):
        k, r = q % 3, q // 3
        rs_recv(q, 2, r3.at[q])
        dims = dims_of(q)
        own = s3[k][piece(s3[k], dims[2], at[dims[2]], [dims[2]], (r,))]
        gsum[:, q * 128 : (q + 1) * 128] = own + r3[q, 0] + r3[q, 1] + r3[q, 2]

    rs_sib(0)
    for q in range(PANELS):
        keep[q] = grad_dot(q, c)
        if q + 1 < PANELS:
            rs_sib(q + 1)
        rs_first(q)
    for q in range(PANELS):
        rs_second(q)
    for q in range(PANELS):
        rs_third(q)
    for q in range(PANELS):
        rs_last(q)

    stream, attn = stream_s[...], attn_s[...]
    inv_attn, inv_stream = nbuf[4, 0][:, :1], nbuf[4, 1][:, :1]
    post, final = pg_ref[:, share], fg_ref[:, share]
    upstream = gsum[...] * final
    cross = z_sum(2, row_sum(stream * upstream))[:, :1]
    grad_stream = inv_stream * (upstream - stream * (inv_stream * inv_stream) * (cross / WIDTH))
    scaled = grad_stream * post
    cross_attn = z_sum(3, row_sum(attn * scaled))[:, :1]
    grad_attn = (inv_attn * (scaled - attn * (inv_attn * inv_attn) * (cross_attn / WIDTH))).astype(BF16)
    for i in range(4):
        gout[i] = grad_attn[:, i * COLS : (i + 1) * COLS]

    def ga_send(i, _):
        xx, zz = i // 4, i % 4
        home = jnp.logical_and(jnp.logical_and(xx == x, zz == z), y == z)

        @pl.when(jnp.logical_not(home))
        def _():
            remote(gout.at[xx], gin.at[p], ga_ss.at[i], ga_rs.at[p], (z * 4 + xx, zz * 2 + c)).start()

        @pl.when(home)
        def _():
            gin[p] = gout[xx]

        return 0

    lax.fori_loop(0, 16, ga_send, 0)
    d_res = grad_stream.astype(BF16)
    left_half, right_half = d_res[:, :576], d_res[:, 576:]
    dsend[...] = jnp.where(c == 0, right_half, left_half)
    dres_copy = remote(dsend, drecv, sib_ss.at[2], sib_rs.at[2], sib)
    dres_copy.start()
    dres_out[rows_of(c * 16, 16), :] = jnp.where(c == 0, left_half, right_half)

    def ga_wait(i, _):
        home = jnp.logical_and(i == p, y == z)

        @pl.when(jnp.logical_not(home))
        def _():
            remote(gin.at[i], gin.at[i], ga_ss.at[0], ga_rs.at[i], (i, y * 2 + c)).wait_recv()

        return 0

    lax.fori_loop(0, 16, ga_wait, 0)
    ga = gin[...].reshape(256, COLS)
    dcs[...] = (
        lax.dot_general(ga, ow[...], (((1,), (1,)), ((), ())), preferred_element_type=F32)
        .astype(BF16)
        .reshape(16, 16, 1024)
    )

    def dc_send(j, _):
        i = peer32(j)
        remote(
            dcs.at[i // 2, :, lanes((i % 2) * 512, 512)], dcr.at[me], dc_ss.at[j], dc_rs.at[j], place32(i)
        ).start()
        return 0

    lax.fori_loop(1, 32, dc_send, 0)
    dcr[me] = dcs[p, :, my_lanes]

    def og_dot(which):
        heads = ctx[:, :, lanes(which * 512, 512)].reshape(256, 512)
        return lax.dot_general(heads, ga, (((0,), (0,)), ((), ())), preferred_element_type=F32)

    ogs[...] = og_dot(1 - c)
    og_copy = remote(ogs, ogr, sib_ss.at[3], sib_rs.at[3], sib)
    og_copy.start()
    og_own = og_dot(c)
    og_copy.wait_recv()
    og_out[...] = (og_own + ogr[...]).astype(BF16)
    dres_copy.wait_recv()
    dres_out[rows_of((1 - c) * 16, 16), :] = drecv[...]

    def dc_wait(j, _):
        i = lax.rem(me + 32 - j, 32)
        remote(dcr.at[i], dcr.at[i], dc_ss.at[j], dc_rs.at[j], place32(i)).wait_recv()
        return 0

    lax.fori_loop(1, 32, dc_wait, 0)
    for cc in range(2):
        total = dcr[cc].astype(F32)
        for i in range(1, 16):
            total = total + dcr[2 * i + cc].astype(F32)
        dctx_out[cc * 16 : (cc + 1) * 16, :] = total.astype(BF16)

    def ctx_sent(j, _):
        src = ctx_ref.at[pl.ds(0, 16)]
        remote(src, src, ctx_ss.at[j], ctx_rs.at[j], sib).wait_send()
        src = dcr.at[0]
        remote(src, src, dc_ss.at[j], dc_rs.at[j], sib).wait_send()
        return 0

    lax.fori_loop(1, 32, ctx_sent, 0)

    def at_sent(i, _):
        @pl.when(jnp.logical_not(jnp.logical_and(i == p, y == z)))
        def _():
            remote(aout.at[i], aout.at[i], at_ss.at[i], at_rs.at[0, 0], sib).wait_send()

        @pl.when(jnp.logical_not(jnp.logical_and(jnp.logical_and(i // 4 == x, i % 4 == z), y == z)))
        def _():
            remote(gout.at[0], gout.at[0], ga_ss.at[i], ga_rs.at[0], sib).wait_send()

        return 0

    lax.fori_loop(0, 16, at_sent, 0)

    def tp_sent(j, _):
        remote(psrc, psrc, tp_ss.at[j], tp_rs.at[j], sib).wait_send()
        return 0

    lax.fori_loop(1, 16, tp_sent, 0)

    def tm_sent(j, _):
        remote(psrc, psrc, tm_ss.at[j], tm_rs.at[j], sib).wait_send()
        return 0

    lax.fori_loop(1, 8, tm_sent, 0)
    ow_copy.wait_send()
    res_copy.wait_send()
    dres_copy.wait_send()
    og_copy.wait_send()
    for which in range(4):
        for by in NEAR:
            remote(nbuf.at[0, 0], nbuf.at[0, 0], z_ss.at[which, by - 1], z_rs.at[which, by - 1], sib).wait_send()
    for q in range(PANELS):
        k, r = q % 3, q // 3
        remote(gath.at[q, c], gath.at[q, c], agc_ss.at[q], agc_rs.at[q], sib).wait_send()
        remote(sib_out.at[q], sib_in.at[q], rc_ss.at[q], rc_rs.at[q], sib).wait_send()
        for by in NEAR:
            for stage in range(3):
                src = region(q, at, GATHER[k][:stage])
                remote(src, src, ag_ss.at[q, stage, by - 1], ag_rs.at[q, stage, by - 1], sib).wait_send()
                src = (r1[k].at[r, 0], r2[k].at[r, 0], r3.at[q, 0])[stage]
                remote(src, src, rs_ss.at[q, stage, by - 1], rs_rs.at[q, stage, by - 1], sib).wait_send()
    n_copy.wait()
    g_copy.wait()


def section_listed(*refs):
    ins, outs, rest = refs[:7], refs[7:13], refs[13:]
    names, n = [], 0
    for count in LAYOUT:
        names.append(rest[n] if count == 1 else tuple(rest[n : n + count]))
        n += count
    section(*ins, *outs, *names)


VM = pltpu.VMEM
DMA = pltpu.SemaphoreType.DMA
SCRATCH = [
    VM((9, 512, 1024), BF16),
    VM((16, 16, 1024), BF16),
    VM((1024, COLS), BF16),
    VM((16, 576), BF16),
    VM((16, 16, COLS), F32),
    VM((4, 4, 16, COLS), F32),
    VM((16, SHARE), F32),
    VM((16, SHARE), F32),
    VM((5, 4, 16, 128), F32),
    VM((9, 2, 4, 4, 16, 512), BF16),
    VM((512, 1024), F32),
    VM((512, 128), jnp.int32),
    VM((512, 128), F32),
    VM((512, 128), F32),
    VM((8, 128), F32),
    VM((16, 8, 128), F32),
    VM((8, 8, 128), F32),
    VM((512, 128), F32),
    VM((512, 1024), BF16),
    VM((9, 4, 4, 16, 512), F32),
    VM((9, 4, 4, 16, 512), BF16),
    VM((9, 4, 4, 16, 512), BF16),
    VM((9, 4, 4, 16, 512), BF16),
    VM((3, 3, 4, 16, 512), BF16),
    VM((3, 3, 4, 4, 16, 128), BF16),
    VM((3, 3, 4, 16, 512), BF16),
    (VM((3, 4, 16, 512), BF16), VM((3, 4, 4, 16, 128), BF16), VM((3, 4, 16, 512), BF16)),
    (VM((3, 4, 16, 512), F32), VM((3, 4, 4, 16, 128), F32), VM((3, 4, 16, 512), F32)),
    VM((3, 3, 16, 512), BF16),
    VM((3, 3, 4, 16, 128), BF16),
    VM((3, 3, 4, 16, 128), BF16),
    (VM((3, 16, 512), F32), VM((3, 4, 16, 128), F32), VM((3, 4, 16, 128), F32)),
    VM((9, 3, 16, 128), F32),
    VM((16, SHARE), F32),
    VM((8, 128), F32),
    VM((4, 16, COLS), BF16),
    VM((16, 16, COLS), BF16),
    VM((16, 16, 1024), BF16),
    VM((32, 16, 512), BF16),
    VM((512, COLS), F32),
    VM((512, COLS), F32),
    VM((16, 576), BF16),
    VM((16, 576), BF16),
    DMA((4,)),
    DMA((32,)), DMA((32,)),
    DMA((4,)), DMA((4,)),
    DMA((16,)), DMA((4, 4)),
    DMA((4, 3)), DMA((4, 3)),
    DMA((9, 3, 3)), DMA((9, 3, 3)),
    DMA((9,)), DMA((9,)),
    DMA((16,)), DMA((16,)),
    DMA((8,)), DMA((8,)),
    DMA((9,)), DMA((9,)),
    DMA((9, 3, 3)), DMA((9, 3, 3)),
    DMA((16,)), DMA((16,)),
    DMA((32,)), DMA((32,)),
    DMA((2,)),
]
LAYOUT = [len(s) if type(s) is tuple else 1 for s in SCRATCH]
FLAT = [t for s in SCRATCH for t in (s if type(s) is tuple else (s,))]


def head_grad_kernel(n_ref, g_ref, loss_in, og_in, dres_in, dctx_in, hg_ref, loss_ref, og_ref, dres_ref, dctx_ref):
    product = lax.dot_general(n_ref[0], g_ref[...], (((0,), (0,)), ((), ())), preferred_element_type=F32)
    hg_ref[...] = product.astype(BF16).reshape(4, 1, 128, 1024)

    @pl.when(pl.program_id(0) == 0)
    def _():
        loss_ref[...] = loss_in[...]
        og_ref[...] = og_in[...]
        dres_ref[...] = dres_in[...]
        dctx_ref[...] = dctx_in[...]


def on_device(context, residual_in, o_weight, post_gain, final_gain, head_weight, targets):
    vmem, hbm = pl.BlockSpec(memory_space=pltpu.VMEM), pl.BlockSpec(memory_space=pl.ANY)
    shape = jax.ShapeDtypeStruct
    small = [shape((1, 1), F32), shape((512, COLS), BF16), shape((32, 576), BF16), shape((32, 512), BF16)]
    normed, grad, loss, og, dres, dctx = pl.pallas_call(
        section_listed,
        out_shape=[shape((9, 2, 4, 4, 16, 512), BF16), shape((512, 1024), BF16), *small],
        in_specs=[vmem, vmem, vmem, vmem, vmem, hbm, vmem],
        out_specs=[hbm, hbm, vmem, vmem, vmem, vmem],
        scratch_shapes=FLAT,
        compiler_params=pltpu.CompilerParams(
            collective_id=0, has_side_effects=True, vmem_limit_bytes=60 * 2**20
        ),
        cost_estimate=pl.CostEstimate(flops=10**10, bytes_accessed=20 * 10**6, transcendentals=10**6),
        name="section",
    )(
        context,
        residual_in,
        o_weight,
        post_gain.reshape(1, WIDTH),
        final_gain.reshape(1, WIDTH),
        head_weight.reshape(4, 9, 128, 1024),
        targets.reshape(4, 128),
    )
    whole = lambda *dims: pl.BlockSpec(dims, lambda q: (0,) * len(dims))
    head_grad, loss, og, dres, dctx = pl.pallas_call(
        head_grad_kernel,
        grid=(9,),
        out_shape=[shape((4, 9, 128, 1024), BF16), *small],
        in_specs=[
            pl.BlockSpec((1, 512, 512), lambda q: (q, 0, 0)),
            whole(512, 1024), whole(1, 1), whole(512, COLS), whole(32, 576), whole(32, 512),
        ],
        out_specs=[
            pl.BlockSpec((4, 1, 128, 1024), lambda q: (0, q, 0, 0)),
            whole(1, 1), whole(512, COLS), whole(32, 576), whole(32, 512),
        ],
        compiler_params=pltpu.CompilerParams(vmem_limit_bytes=48 * 2**20),
        cost_estimate=pl.CostEstimate(flops=5 * 10**9, bytes_accessed=16 * 10**6, transcendentals=0),
        name="head_grad",
    )(normed.reshape(9, 512, 512), grad, loss, og, dres, dctx)
    return (loss.reshape(()), head_grad.reshape(WIDTH, 1024), og, dres, dctx)


def solution(mesh):
    placed = (
        P("pipe", "mp"),
        P("pipe", "mp"),
        P("mp", "pipe"),
        P(),
        P(),
        P(None, ("pipe", "mp")),
        P(),
    )
    return jax.shard_map(
        on_device,
        mesh=mesh,
        in_specs=placed,
        out_specs=(P(), P(None, ("pipe", "mp")), P("mp", "pipe"), P("pipe", "mp"), P("pipe", "mp")),
        check_vma=False,
    )
```

```python
import jax
import jax.numpy as jnp
from jax import lax
from jax.experimental import pallas as pl
from jax.experimental.pallas import tpu as pltpu
from jax.sharding import PartitionSpec as P

epsilon = 1e-06
softcap = 30.0
MESH = pl.DeviceIdType.MESH
F32, BF16 = jnp.float32, jnp.bfloat16

WIDTH = 4608
SHARE = 1152
PANELS = 9
CHUNK = 8
EARLY = 4
COLS = 288
GATHER = (("y", "x", "z"), ("x", "z", "y"), ("z", "y", "x"))
NEAR = (1, 3, 2)


def remote(src, dst, send, recv, device):
    return pltpu.make_async_remote_copy(
        src_ref=src, dst_ref=dst, send_sem=send, recv_sem=recv, device_id=device, device_id_type=MESH
    )


def place(at):
    return (at["y"] * 4 + at["x"], at["z"] * 2 + at["c"])


def moved(at, dim, by):
    size = 2 if dim == "c" else 4
    return {**at, dim: lax.rem(at[dim] + by, size)}


def lanes(start, size):
    return pl.ds(pl.multiple_of(start, 128), size)


def rows_of(start, size):
    return pl.ds(pl.multiple_of(start, 16), size)


def section(
    ctx_ref, res_ref, ow_ref, pg_ref, fg_ref, w_hbm, tgt_ref,
    n_out, g_out, x_out, loss_out, og_out, dres_out, dctx_out,
    wv, ctx, ow, pg, fg, rres, aout, ain, attn_s, stream_s, nbuf, gath, turned_q, cap, tgt, hot, part,
    psrc, pipe_in, mp_in, scale, grad, early,
    keep, sib_out, sib_in, first, r1a, r1b, r1c, s2, own2, r2a, r2b, r2c, s3, r3,
    gsum, gout, gin, dcs, dcr, ogs, ogr, dsend, drecv,
    w_sem, ctx_ss, ctx_rs, sib_ss, sib_rs, tn_ss, tn_rs, at_ss, at_rs, y_ss, y_rs, ag_ss, ag_rs, agc_ss, agc_rs, tp_ss, tp_rs, tm_ss, tm_rs,
    rc_ss, rc_rs, rs_ss, rs_rs, ga_ss, ga_rs, dc_ss, dc_rs, out_sem, early_sem,
):
    p, m = lax.axis_index("pipe"), lax.axis_index("mp")
    y, x, z, c = p // 4, p % 4, m // 2, m % 2
    at = {"y": y, "x": x, "z": z, "c": c}
    sib = (p, z * 2 + (1 - c))
    me = p * 2 + c
    peer32 = lambda j: lax.rem(me + j, 32)
    place32 = lambda i: (i // 2, z * 2 + i % 2)

    w_copies = [
        pltpu.make_async_copy(w_hbm.at[i], wv.at[:, pl.ds(i * 128, 128), :], w_sem) for i in range(4)
    ]
    for copy in w_copies:
        copy.start()

    pending = []

    def finish():
        for wait in pending:
            wait()

    def landed(like, sem):
        remote(like, like, sem, sem, sib).wait_recv()

    def gone(like, sem):
        pending.append(remote(like, like, sem, sem, sib).wait_send)

    barrier = pltpu.get_barrier_semaphore()

    def greet(device):
        pl.semaphore_signal(barrier, inc=1, device_id=device, device_id_type=MESH)

    def greet32(j, _):
        greet(place32(peer32(j)))
        return 0

    lax.fori_loop(1, 32, greet32, 0)
    for by in (1, 2, 3):
        zz = lax.rem(z + by, 4)
        greet((p, zz * 2 + (1 - c)))
        for xx in range(4):
            greet((y * 4 + xx, zz * 2 + c))
    turned = (z * 4 + x, y * 2)

    @pl.when(y != z)
    def _():
        for cc in range(2):
            greet((turned[0], turned[1] + cc))

    pl.semaphore_wait(barrier, 46 + 2 * jnp.where(y != z, 1, 0))

    my_lanes = lanes(c * 512, 512)

    def ctx_copy(by, h):
        there = lax.rem(p + by, 16)
        src = ctx_ref.at[rows_of(h * 16, 16)]
        return remote(src, ctx.at[p, :, my_lanes], ctx_ss.at[0], ctx_rs.at[by // CHUNK], (there, z * 2 + h))

    def ctx_send(by, _):
        for h in range(2):
            ctx_copy(by, h).start()
        return 0

    ctx_home = remote(
        ctx_ref.at[rows_of((1 - c) * 16, 16)], ctx.at[p, :, my_lanes], sib_ss.at[2], sib_rs.at[2], sib
    )
    ctx_home.start()
    pending.append(ctx_home.wait_send)
    ow_copy = remote(ow_ref, ow.at[:, my_lanes], sib_ss.at[0], sib_rs.at[0], sib)
    ow_copy.start()
    pending.append(ow_copy.wait_send)
    lax.fori_loop(1, 16, ctx_send, 0)
    gone(ctx.at[pl.ds(0, 15)], ctx_ss.at[0])

    def turn(sources, landing, base):
        def at_home(cc):
            return jnp.logical_and(y == z, c == cc)

        for cc in range(2):
            copy = remote(
                sources[cc], landing.at[c], tn_ss.at[base, cc], tn_rs.at[base, c], (turned[0], turned[1] + cc)
            )
            pl.when(jnp.logical_not(at_home(cc)))(copy.start)

            @pl.when(at_home(cc))
            def _(cc=cc):
                landing[cc] = sources[cc][...]

            pending.append(lambda cc=cc, copy=copy: pl.when(jnp.logical_not(at_home(cc)))(copy.wait_send))

        def receive():
            for cc in range(2):
                copy = remote(
                    landing.at[cc], landing.at[cc], tn_ss.at[base, cc], tn_rs.at[base, cc], (turned[0], turned[1] + cc)
                )
                pl.when(jnp.logical_not(at_home(cc)))(copy.wait_recv)

        return receive

    res_receive = turn([res_ref.at[pl.ds(cc * 16, 16)] for cc in range(2)], rres, 0)
    ctx[p, :, my_lanes] = ctx_ref[rows_of(c * 16, 16), :]
    ow[:, my_lanes] = ow_ref[...]
    pg[...] = pg_ref[...].reshape(1, WIDTH)
    fg[...] = fg_ref[...].reshape(1, WIDTH)
    for i in range(4):
        block = jnp.broadcast_to(tgt_ref[i : i + 1, :], (128, 128)).T
        for j in range(4):
            for cc in range(2):
                tgt[cc * 256 + (i * 4 + j) * 16 : cc * 256 + (i * 4 + j + 1) * 16, :] = block[
                    j * 32 + cc * 16 : j * 32 + (cc + 1) * 16, :
                ]

    ctx_there = ctx.at[p, :, lanes((1 - c) * 512, 512)]
    landed(ctx_there, sib_rs.at[2])
    ow_there = ow.at[:, lanes((1 - c) * 512, 512)]
    landed(ow_there, sib_rs.at[0])

    group = z * 4 + x
    place16 = lambda g: (y * 4 + g % 4, (g // 4) * 2 + c)

    def attn_copy(g):
        return remote(aout.at[g], ain.at[group], at_ss, at_rs, place16(g))

    for chunk in range(0, 16, CHUNK):
        landed(ctx.at[pl.ds(0, CHUNK - (chunk == 0))], ctx_rs.at[chunk // CHUNK])
        groups = [lax.rem(p + 16 - by, 16) for by in range(chunk, chunk + CHUNK)]
        sums = lax.dot_general(
            jnp.concatenate([ctx[g] for g in groups], axis=0), ow[...], (((1,), (1,)), ((), ())), preferred_element_type=F32
        )
        for i, g in enumerate(groups):
            aout[g] = sums[i * 16 : (i + 1) * 16]
            pl.when(g != group)(attn_copy(g).start)
    gone(aout.at[pl.ds(0, 15)], at_ss)
    ain[group] = aout[group]
    res_receive()
    landed(ain.at[pl.ds(0, 15)], at_rs)
    attn = jnp.concatenate([ain[i] + ain[4 + i] + ain[8 + i] + ain[12 + i] for i in range(4)], axis=1)
    residual = jnp.concatenate([rres[0], rres[1]], axis=1).astype(F32)
    share = lanes(y * SHARE, SHARE)
    post, final = pg[:, share], fg[:, share]

    def y_sum(which, values):
        lane = lax.broadcasted_iota(jnp.int32, (16, 128), 1)
        packed = jnp.zeros((16, 128), F32)
        for i, value in enumerate(values):
            packed = jnp.where(lane == i, jnp.sum(value, axis=1, keepdims=True), packed)
        nbuf[which, y] = packed
        for by in NEAR:
            remote(
                nbuf.at[which, y], nbuf.at[which, y], y_ss.at[which], y_rs.at[which], place(moved(at, "y", by))
            ).start()
        gone(nbuf.at[which, pl.ds(0, 3)], y_ss.at[which])
        landed(nbuf.at[which, pl.ds(0, 3)], y_rs.at[which])
        total = nbuf[which, 0] + nbuf[which, 1] + nbuf[which, 2] + nbuf[which, 3]
        return [total[:, i : i + 1] for i in range(len(values))]

    gained = attn * post
    attn_sq, res_sq, mixed, gained_sq = y_sum(0, [attn * attn, residual * residual, residual * gained, gained * gained])
    inv_attn = lax.rsqrt(attn_sq / WIDTH + epsilon)
    stream = residual + attn * inv_attn * post
    stream_sq = jnp.maximum(res_sq + 2.0 * inv_attn * mixed + inv_attn * inv_attn * gained_sq, 0.0)
    inv_stream = lax.rsqrt(stream_sq / WIDTH + epsilon)
    normed = (stream * inv_stream * final).astype(BF16)
    attn_s[...] = attn
    stream_s[...] = stream
    nbuf[2, 0] = jnp.broadcast_to(inv_attn, (16, 128))
    nbuf[2, 1] = jnp.broadcast_to(inv_stream, (16, 128))

    my_y = lanes(y * 128, 128)
    for q in range(PANELS):
        gath[q, c, z, x, :, my_y] = normed[:, q * 128 : (q + 1) * 128]

    def region(q, here, done):
        return gath.at[
            q,
            here["c"],
            pl.ds(0, 4) if "z" in done else here["z"],
            pl.ds(0, 4) if "x" in done else here["x"],
            :,
            pl.ds(0, 512) if "y" in done else lanes(here["y"] * 128, 128),
        ]

    def ag_start(q, stage):
        dims = GATHER[q % 3]
        src = region(q, at, dims[:stage])
        for by in NEAR:
            remote(src, src, ag_ss.at[stage], ag_rs.at[q, stage], place(moved(at, dims[stage], by))).start()

    def three_regions(q, stage):
        if stage == 0:
            return gath.at[q, c, 0, pl.ds(0, 3), :, pl.ds(0, 128)]
        if stage == 1:
            return gath.at[q, c, pl.ds(0, 3), :, :, pl.ds(0, 128)]
        return gath.at[q, c, pl.ds(0, 3)]

    def ag_wait(q, stage):
        landed(three_regions(q, stage), ag_rs.at[q, stage])

    for q in range(PANELS):
        ag_start(q, 0)
    for stage in (1, 2):
        for q in range(PANELS):
            ag_wait(q, stage - 1)
            ag_start(q, stage)
    pltpu.make_async_copy(wv, wv, w_sem).wait()

    def logits(third, which):
        rows = lambda: rows_of(which * 256, 256)

        @pl.loop(0, 4)
        def _(block):
            cols = lanes(block * 256, 256)
            total = None
            for q in range(third * 3, third * 3 + 3):
                term = jnp.dot(gath[q, which].reshape(256, 512), wv[q, :, cols], preferred_element_type=F32)
                total = term if total is None else total + term
            if third > 0:
                total = total + cap[rows(), cols]
            if third < 2:
                cap[rows(), cols] = total
            else:
                capped = softcap * jnp.tanh(total * (1.0 / softcap))
                cap[rows(), cols] = capped
                expd = jnp.exp(capped)
                first_col = m * 1024 + p * 8192 + block * 256
                ids = lax.broadcasted_iota(jnp.int32, (256, 128), 1) + first_col
                wanted = tgt[rows(), :]
                sums = expd[:, :128] + expd[:, 128:]
                hits = jnp.where(ids == wanted, capped[:, :128], 0.0) + jnp.where(
                    ids + 128 == wanted, capped[:, 128:], 0.0
                )

                @pl.when(block == 0)
                def _():
                    part[rows(), :] = sums
                    hot[rows(), :] = hits

                @pl.when(block > 0)
                def _():
                    part[rows(), :] += sums
                    hot[rows(), :] += hits

    for stage in range(3):
        gone(three_regions(pl.ds(0, PANELS), stage), ag_ss.at[stage])
    for third in range(3):
        panels = pl.ds(third * 3, 3)
        for q in range(third * 3, third * 3 + 3):
            ag_wait(q, 2)
        remote(gath.at[panels, c], gath.at[panels, c], agc_ss, agc_rs.at[third], sib).start()
        logits(third, c)
        landed(gath.at[panels, 1 - c], agc_rs.at[third])
        logits(third, 1 - c)
    gone(gath.at[:, c], agc_ss)

    for i in range(4):
        psrc[i : i + 1, :] = jnp.sum(part[i * 128 : (i + 1) * 128, :].T, axis=0, keepdims=True)
        psrc[i + 4 : i + 5, :] = jnp.sum(hot[i * 128 : (i + 1) * 128, :].T, axis=0, keepdims=True)
    pipe_in[p] = psrc[...]

    def pipe_send(j, _):
        remote(psrc, pipe_in.at[p], tp_ss, tp_rs, (lax.rem(p + j, 16), m)).start()
        return 0

    lax.fori_loop(1, 16, pipe_send, 0)
    gone(pipe_in.at[pl.ds(0, 15)], tp_ss)

    @pl.loop(0, PANELS)
    def _(q):
        turned_q[q] = gath[q].reshape(512, 512).T

    n_copy = pltpu.make_async_copy(turned_q, n_out, out_sem.at[0])
    n_copy.start()
    pending.append(n_copy.wait)
    landed(pipe_in.at[pl.ds(0, 15)], tp_rs)
    mp_in[m] = jnp.sum(pipe_in[...], axis=0)

    def mp_send(j, _):
        remote(mp_in.at[m], mp_in.at[m], tm_ss, tm_rs, (p, lax.rem(m + j, 8))).start()
        return 0

    lax.fori_loop(1, 8, mp_send, 0)
    gone(mp_in.at[pl.ds(0, 7)], tm_ss)
    landed(mp_in.at[pl.ds(0, 7)], tm_rs)
    sums = jnp.sum(mp_in[...], axis=0)
    totals, target_logit = sums[:4], sums[4:]
    loss_out[...] = jnp.sum(
        jnp.sum(jnp.log(totals) - target_logit, axis=0, keepdims=True), axis=1, keepdims=True
    ) * (1.0 / 512)
    inverse = 1.0 / totals
    for i in range(4):
        scale[i * 128 : (i + 1) * 128, :] = jnp.broadcast_to(inverse[i : i + 1, :], (128, 128)).T

    @pl.loop(0, 16)
    def _(block):
        rows = rows_of(block * 32, 32)
        wanted, inv = tgt[rows, :], scale[rows, :]
        ids = lax.broadcasted_iota(jnp.int32, (32, 128), 1) + (m * 1024 + p * 8192)
        for j in range(8):
            cols = slice(j * 128, (j + 1) * 128)
            capped = cap[rows, cols]
            ratio = capped * (1.0 / softcap)
            hit = jnp.where(ids + j * 128 == wanted, 1.0, 0.0)
            grad[rows, cols] = ((jnp.exp(capped) * inv - hit) * (1.0 - ratio * ratio)).astype(BF16)

    g_copy = pltpu.make_async_copy(grad, g_out, out_sem.at[1])
    g_copy.start()
    pending.append(g_copy.wait)

    def grad_dot(q, which):
        rows = rows_of(which * 256, 256)
        return lax.dot_general(grad[rows, :], wv[q], (((1,), (1,)), ((), ())), preferred_element_type=F32).reshape(
            4, 4, 16, 512
        )

    def rs_sib(q):
        sib_out[q] = grad_dot(q, 1 - c).astype(BF16)
        remote(sib_out.at[q], sib_in.at[q], rc_ss, rc_rs.at[q], sib).start()

    def piece(ref, dim, index, left, lead):
        where = list(lead)
        for d in ("z", "x"):
            if d in left:
                where.append(index if d == dim else pl.ds(0, 4))
        where.append(pl.ds(0, 16))
        if "y" in left:
            where.append(lanes(index * 128, 128) if dim == "y" else pl.ds(0, 512))
        else:
            where.append(pl.ds(0, 128))
        return tuple(where)

    r1 = (r1a, r1b, r1c)
    r2 = (r2a, r2b, r2c)
    dims_of = lambda q: GATHER[q % 3][::-1]

    def rs_first(q):
        landed(sib_in.at[q], rc_rs.at[q])
        total = keep[q] + sib_in[q].astype(F32)
        keep[q] = total
        first[q] = total.astype(BF16)
        dim = dims_of(q)[0]
        for by in NEAR:
            there = moved(at, dim, by)
            src = first.at[piece(first, dim, there[dim], ("z", "x", "y"), (q,))]
            remote(src, r1[q % 3].at[q // 3, by - 1], rs_ss.at[q % 3, 0], rs_rs.at[q, 0], place(there)).start()

    def rs_second(q):
        k, r = q % 3, q // 3
        got = r1[k].at[r]
        landed(got, rs_rs.at[q, 0])
        dims = dims_of(q)
        left = [d for d in ("z", "x", "y") if d != dims[0]]
        total = keep[piece(keep, dims[0], at[dims[0]], ("z", "x", "y"), (q,))]
        total = total + got[0].astype(F32) + got[1].astype(F32) + got[2].astype(F32)
        own2[k][r] = total
        s2[k][r] = total.astype(BF16)
        for by in NEAR:
            there = moved(at, dims[1], by)
            src = s2[k].at[piece(s2[k], dims[1], there[dims[1]], left, (r,))]
            remote(src, r2[k].at[r, by - 1], rs_ss.at[q % 3, 1], rs_rs.at[q, 1], place(there)).start()

    def rs_third(q):
        k, r = q % 3, q // 3
        got = r2[k].at[r]
        landed(got, rs_rs.at[q, 1])
        dims = dims_of(q)
        left = [d for d in ("z", "x", "y") if d != dims[0]]
        total = own2[k][piece(own2[k], dims[1], at[dims[1]], left, (r,))]
        total = total + got[0].astype(F32) + got[1].astype(F32) + got[2].astype(F32)
        s3[k][r] = total
        for by in NEAR:
            there = moved(at, dims[2], by)
            src = s3[k].at[piece(s3[k], dims[2], there[dims[2]], [dims[2]], (r,))]
            remote(src, r3.at[q, by - 1], rs_ss.at[q % 3, 2], rs_rs.at[q, 2], place(there)).start()

    def rs_last(q):
        k, r = q % 3, q // 3
        landed(r3.at[q], rs_rs.at[q, 2])
        dims = dims_of(q)
        own = s3[k][piece(s3[k], dims[2], at[dims[2]], [dims[2]], (r,))]
        gsum[:, q * 128 : (q + 1) * 128] = own + r3[q, 0] + r3[q, 1] + r3[q, 2]

    def head_early(q):
        early[q] = jnp.dot(turned_q[q], grad[...], preferred_element_type=F32).astype(BF16).reshape(4, 128, 1024)
        copy = pltpu.make_async_copy(early.at[q], x_out.at[q], early_sem.at[q])
        copy.start()
        pending.append(copy.wait)

    rs_sib(0)
    for q in range(PANELS):
        keep[q] = grad_dot(q, c)
        if q + 1 < PANELS:
            rs_sib(q + 1)
        rs_first(q)
    for q in range(PANELS):
        if q % 2 == 0 and q // 2 < EARLY:
            head_early(q // 2)
        rs_second(q)
    for q in range(PANELS):
        rs_third(q)
    for q in range(PANELS):
        rs_last(q)
    gone(sib_out, rc_ss)
    for k in range(3):
        gone(r1[k], rs_ss.at[k, 0])
        gone(r2[k], rs_ss.at[k, 1])
        gone(r3.at[pl.ds(0, 3)], rs_ss.at[k, 2])

    stream, attn = stream_s[...], attn_s[...]
    inv_attn, inv_stream = nbuf[2, 0][:, :1], nbuf[2, 1][:, :1]
    post, final = pg[:, share], fg[:, share]
    upstream = gsum[...] * final
    gained = attn * post
    cross, cross_up, cross_stream = y_sum(1, [stream * upstream, gained * upstream, gained * stream])
    factor = inv_stream * inv_stream * (cross / WIDTH)
    grad_stream = inv_stream * (upstream - stream * factor)
    cross_attn = inv_stream * (cross_up - factor * cross_stream)
    grad_attn = (inv_attn * (grad_stream * post - attn * (inv_attn * inv_attn) * (cross_attn / WIDTH))).astype(BF16)
    for i in range(4):
        gout[i] = grad_attn[:, i * COLS : (i + 1) * COLS]

    def ga_send(j, _):
        g = lax.rem(group + j, 16)
        remote(gout.at[g % 4], gin.at[group], ga_ss, ga_rs, place16(g)).start()
        return 0

    lax.fori_loop(1, 16, ga_send, 0)
    gone(gin.at[pl.ds(0, 15)], ga_ss)
    gin[group] = gout[x]
    d_res = grad_stream.astype(BF16)
    dsend[0] = d_res[:, :576]
    dsend[1] = d_res[:, 576:]
    dres_receive = turn([dsend.at[0], dsend.at[1]], drecv, 1)
    landed(gin.at[pl.ds(0, 15)], ga_rs)
    ga = gin[...].reshape(256, COLS)
    dcs[...] = jnp.dot(ga, ow[...], preferred_element_type=F32).astype(BF16).reshape(16, 16, 1024)

    def dc_send(j, _):
        i = peer32(j)
        remote(
            dcs.at[i // 2, :, lanes((i % 2) * 512, 512)], dcr.at[me], dc_ss, dc_rs, place32(i)
        ).start()
        return 0

    lax.fori_loop(1, 32, dc_send, 0)
    dcr[me] = dcs[p, :, my_lanes]

    def og_dot(which):
        heads = ctx[:, :, lanes(which * 512, 512)].reshape(256, 512)
        return lax.dot_general(ga, heads, (((0,), (0,)), ((), ())), preferred_element_type=F32)

    ogs[...] = og_dot(1 - c)
    og_copy = remote(ogs, ogr, sib_ss.at[1], sib_rs.at[1], sib)
    og_copy.start()
    og_own = og_dot(c)
    og_copy.wait_recv()
    og_out[...] = (og_own + ogr[...]).astype(BF16)
    dres_receive()
    for cc in range(2):
        dres_out[cc * 16 : (cc + 1) * 16, :] = drecv[cc]

    finish()
    og_copy.wait_send()

    landed(dcr.at[pl.ds(0, 31)], dc_rs)
    remote(dcr.at[pl.ds(0, 31)], dcr.at[pl.ds(0, 31)], dc_ss, dc_rs, sib).wait_send()
    for cc in range(2):
        total = dcr[cc].astype(F32)
        for i in range(1, 16):
            total = total + dcr[2 * i + cc].astype(F32)
        dctx_out[cc * 16 : (cc + 1) * 16, :] = total.astype(BF16)


def section_listed(*refs):
    ins, outs, rest = refs[:7], refs[7:14], refs[14:]
    names, n = [], 0
    for count in LAYOUT:
        names.append(rest[n] if count == 1 else tuple(rest[n : n + count]))
        n += count
    section(*ins, *outs, *names)


VM = pltpu.VMEM
DMA = pltpu.SemaphoreType.DMA
SCRATCH = [
    VM((9, 512, 1024), BF16),
    VM((16, 16, 1024), BF16),
    VM((COLS, 1024), BF16),
    VM((1, WIDTH), F32),
    VM((1, WIDTH), F32),
    VM((2, 16, 576), BF16),
    VM((16, 16, COLS), F32),
    VM((16, 16, COLS), F32),
    VM((16, SHARE), F32),
    VM((16, SHARE), F32),
    VM((3, 4, 16, 128), F32),
    VM((9, 2, 4, 4, 16, 512), BF16),
    VM((9, 512, 512), BF16),
    VM((512, 1024), F32),
    VM((512, 128), jnp.int32),
    VM((512, 128), F32),
    VM((512, 128), F32),
    VM((8, 128), F32),
    VM((16, 8, 128), F32),
    VM((8, 8, 128), F32),
    VM((512, 128), F32),
    VM((512, 1024), BF16),
    VM((EARLY, 4, 128, 1024), BF16),
    VM((9, 4, 4, 16, 512), F32),
    VM((9, 4, 4, 16, 512), BF16),
    VM((9, 4, 4, 16, 512), BF16),
    VM((9, 4, 4, 16, 512), BF16),
    VM((3, 3, 4, 16, 512), BF16),
    VM((3, 3, 4, 4, 16, 128), BF16),
    VM((3, 3, 4, 16, 512), BF16),
    (VM((3, 4, 16, 512), BF16), VM((3, 4, 4, 16, 128), BF16), VM((3, 4, 16, 512), BF16)),
    (VM((3, 4, 16, 512), F32), VM((3, 4, 4, 16, 128), F32), VM((3, 4, 16, 512), F32)),
    VM((3, 3, 16, 512), BF16),
    VM((3, 3, 4, 16, 128), BF16),
    VM((3, 3, 4, 16, 128), BF16),
    (VM((3, 16, 512), F32), VM((3, 4, 16, 128), F32), VM((3, 4, 16, 128), F32)),
    VM((9, 3, 16, 128), F32),
    VM((16, SHARE), F32),
    VM((4, 16, COLS), BF16),
    VM((16, 16, COLS), BF16),
    VM((16, 16, 1024), BF16),
    VM((32, 16, 512), BF16),
    VM((COLS, 512), F32),
    VM((COLS, 512), F32),
    VM((2, 16, 576), BF16),
    VM((2, 16, 576), BF16),
    DMA,
    DMA((1,)), DMA((16 // CHUNK,)),
    DMA((3,)), DMA((3,)),
    DMA((2, 2)), DMA((2, 2)),
    DMA, DMA,
    DMA((2,)), DMA((2,)),
    DMA((3,)), DMA((9, 3)),
    DMA, DMA((3,)),
    DMA, DMA,
    DMA, DMA,
    DMA, DMA((9,)),
    DMA((3, 3)), DMA((9, 3)),
    DMA, DMA,
    DMA, DMA,
    DMA((2,)),
    DMA((EARLY,)),
]
LAYOUT = [len(s) if type(s) is tuple else 1 for s in SCRATCH]
FLAT = [t for s in SCRATCH for t in (s if type(s) is tuple else (s,))]


def head_grad_kernel(
    n_hbm, g_hbm, x_hbm, loss_in, og_in, dres_in, dctx_in, hg_hbm, loss_ref, og_out, dres_out, dctx_out,
    n_buf, g_buf, x_buf, out_buf, og_buf, dres_buf, dctx_buf, n_sem, g_sem, x_sem, out_sem, small_sem,
):
    panels = range(EARLY, PANELS)
    g_copy = pltpu.make_async_copy(g_hbm, g_buf, g_sem)
    n_copies = {q: pltpu.make_async_copy(n_hbm.at[q], n_buf.at[q - EARLY], n_sem.at[q - EARLY]) for q in panels}
    x_copies = [pltpu.make_async_copy(x_hbm.at[q], x_buf.at[q], x_sem.at[q]) for q in range(EARLY)]
    small = ((og_in, og_buf, og_out), (dres_in, dres_buf, dres_out), (dctx_in, dctx_buf, dctx_out))
    small_in = [pltpu.make_async_copy(a, b, small_sem.at[0, i]) for i, (a, b, _) in enumerate(small)]
    small_out = [pltpu.make_async_copy(b, a, small_sem.at[1, i]) for i, (_, b, a) in enumerate(small)]
    g_copy.start()
    for i, q in enumerate(panels):
        n_copies[q].start()
        if i < EARLY:
            x_copies[i].start()
    for copy in small_in:
        copy.start()
    loss_ref[...] = loss_in[...]
    g_copy.wait()
    outs = []

    def write(source, q):
        copy = pltpu.make_async_copy(source, hg_hbm.at[:, q], out_sem.at[q])
        copy.start()
        outs.append(copy)

    for i, q in enumerate(panels):
        n_copies[q].wait()
        product = jnp.dot(n_buf[i], g_buf[...], preferred_element_type=F32)
        out_buf[i] = product.astype(BF16).reshape(4, 128, 1024)
        write(out_buf.at[i], q)
        if i < EARLY:
            x_copies[i].wait()
            write(x_buf.at[i], i)
    for one, two in zip(small_in, small_out):
        one.wait()
        two.start()
    for copy in outs + small_out:
        copy.wait()


def on_device(context, residual_in, o_weight, post_gain, final_gain, head_weight, targets):
    vmem, hbm = pl.BlockSpec(memory_space=pltpu.VMEM), pl.BlockSpec(memory_space=pl.ANY)
    shape = jax.ShapeDtypeStruct
    small = [shape((1, 1), F32), shape((COLS, 512), BF16), shape((32, 576), BF16), shape((32, 512), BF16)]
    normed, grad, early, loss, og, dres, dctx = pl.pallas_call(
        section_listed,
        out_shape=[shape((9, 512, 512), BF16), shape((512, 1024), BF16), shape((EARLY, 4, 128, 1024), BF16), *small],
        in_specs=[vmem, vmem, vmem, vmem, vmem, hbm, vmem],
        out_specs=[hbm, hbm, hbm, vmem, vmem, vmem, vmem],
        scratch_shapes=FLAT,
        compiler_params=pltpu.CompilerParams(
            collective_id=0, has_side_effects=True, vmem_limit_bytes=60 * 2**20
        ),
        cost_estimate=pl.CostEstimate(flops=10**10, bytes_accessed=20 * 10**6, transcendentals=10**6),
        name="section",
    )(
        context,
        residual_in,
        o_weight.T,
        post_gain,
        final_gain,
        head_weight.reshape(4, 9, 128, 1024),
        targets.reshape(4, 128),
    )
    rest = PANELS - EARLY
    head_grad, loss, og, dres, dctx = pl.pallas_call(
        head_grad_kernel,
        out_shape=[shape((4, 9, 128, 1024), BF16), *small],
        in_specs=[hbm, hbm, hbm, vmem, hbm, hbm, hbm],
        out_specs=[hbm, vmem, hbm, hbm, hbm],
        scratch_shapes=[
            VM((rest, 512, 512), BF16), VM((512, 1024), BF16), VM((EARLY, 4, 128, 1024), BF16),
            VM((rest, 4, 128, 1024), BF16), VM((COLS, 512), BF16), VM((32, 576), BF16), VM((32, 512), BF16),
            DMA((rest,)), DMA, DMA((EARLY,)), DMA((PANELS,)), DMA((2, 3)),
        ],
        compiler_params=pltpu.CompilerParams(vmem_limit_bytes=60 * 2**20),
        cost_estimate=pl.CostEstimate(flops=3 * 10**9, bytes_accessed=18 * 10**6, transcendentals=0),
        name="head_grad",
    )(normed, grad, early, loss, og, dres, dctx)
    return (loss.reshape(()), head_grad.reshape(WIDTH, 1024), og.T, dres, dctx)


def solution(mesh):
    placed = (
        P("pipe", "mp"),
        P("pipe", "mp"),
        P("mp", "pipe"),
        P(),
        P(),
        P(None, ("pipe", "mp")),
        P(),
    )
    return jax.shard_map(
        on_device,
        mesh=mesh,
        in_specs=placed,
        out_specs=(P(), P(None, ("pipe", "mp")), P("mp", "pipe"), P("pipe", "mp"), P("pipe", "mp")),
        check_vma=False,
    )
```

```python
import jax
import jax.numpy as jnp
from jax import lax
from jax.experimental import pallas as pl
from jax.experimental.pallas import tpu as pltpu
from jax.sharding import PartitionSpec as P

epsilon = 1e-06
softcap = 30.0
MESH = pl.DeviceIdType.MESH
F32, BF16 = jnp.float32, jnp.bfloat16

WIDTH = 4608
SHARE = 1152
PANELS = 9
CHUNK = 8
COLS = 288
GATHER = (("y", "x", "z"), ("x", "z", "y"), ("z", "y", "x"))
NEAR = (1, 3, 2)


def remote(src, dst, send, recv, device):
    return pltpu.make_async_remote_copy(
        src_ref=src, dst_ref=dst, send_sem=send, recv_sem=recv, device_id=device, device_id_type=MESH
    )


def place(at):
    return (at["y"] * 4 + at["x"], at["z"] * 2 + at["c"])


def moved(at, dim, by):
    size = 2 if dim == "c" else 4
    return {**at, dim: lax.rem(at[dim] + by, size)}


def lanes(start, size):
    return pl.ds(pl.multiple_of(start, 128), size)


def rows_of(start, size):
    return pl.ds(pl.multiple_of(start, 16), size)


def section(
    ctx_ref, res_ref, ow_ref, pg_ref, fg_ref, w_hbm, tgt_ref,
    x_out, loss_out, og_out, dres_out, dctx_out,
    wv, ctx, ow, pg, fg, rres, aout, ain, attn_s, stream_s, nbuf, gath, turned_q, cap, tgt, hot, part,
    psrc, pipe_in, mp_in, scale, aim, grad,
    keep, sib_out, sib_in, first, r1a, r1b, r1c, s2, own2, r2a, r2b, r2c, s3, r3,
    gsum, gout, gin, dcs, dcr, ogs, ogr, dsend, drecv,
    w_sem, ctx_ss, ctx_rs, sib_ss, sib_rs, tn_ss, tn_rs, at_ss, at_rs, y_ss, y_rs, ag_ss, ag_rs, agc_ss, agc_rs, tp_ss, tp_rs, tm_ss, tm_rs,
    rc_ss, rc_rs, rs_ss, rs_rs, ga_ss, ga_rs, dc_ss, dc_rs,
):
    p, m = lax.axis_index("pipe"), lax.axis_index("mp")
    y, x, z, c = p // 4, p % 4, m // 2, m % 2
    at = {"y": y, "x": x, "z": z, "c": c}
    sib = (p, z * 2 + (1 - c))
    me = p * 2 + c
    peer32 = lambda j: lax.rem(me + j, 32)
    place32 = lambda i: (i // 2, z * 2 + i % 2)

    w_copies = [
        pltpu.make_async_copy(w_hbm.at[i], wv.at[:, pl.ds(i * 128, 128), :], w_sem) for i in range(4)
    ]
    for copy in w_copies:
        copy.start()

    pending = []

    def finish():
        for wait in pending:
            wait()

    def landed(like, sem):
        remote(like, like, sem, sem, sib).wait_recv()

    def gone(like, sem):
        pending.append(remote(like, like, sem, sem, sib).wait_send)

    barrier = pltpu.get_barrier_semaphore()

    def greet(device):
        pl.semaphore_signal(barrier, inc=1, device_id=device, device_id_type=MESH)

    def greet32(j, _):
        greet(place32(peer32(j)))
        return 0

    lax.fori_loop(1, 32, greet32, 0)
    for by in (1, 2, 3):
        zz = lax.rem(z + by, 4)
        greet((p, zz * 2 + (1 - c)))
        for xx in range(4):
            greet((y * 4 + xx, zz * 2 + c))
    turned = (z * 4 + x, y * 2)

    @pl.when(y != z)
    def _():
        for cc in range(2):
            greet((turned[0], turned[1] + cc))

    pl.semaphore_wait(barrier, 46 + 2 * jnp.where(y != z, 1, 0))

    my_lanes = lanes(c * 512, 512)

    def ctx_copy(by, h):
        there = lax.rem(p + by, 16)
        src = ctx_ref.at[rows_of(h * 16, 16)]
        return remote(src, ctx.at[p, :, my_lanes], ctx_ss.at[0], ctx_rs.at[by // CHUNK], (there, z * 2 + h))

    def ctx_send(by, _):
        for h in range(2):
            ctx_copy(by, h).start()
        return 0

    ctx_home = remote(
        ctx_ref.at[rows_of((1 - c) * 16, 16)], ctx.at[p, :, my_lanes], sib_ss.at[2], sib_rs.at[2], sib
    )
    ctx_home.start()
    pending.append(ctx_home.wait_send)
    ow_copy = remote(ow_ref, ow.at[:, my_lanes], sib_ss.at[0], sib_rs.at[0], sib)
    ow_copy.start()
    pending.append(ow_copy.wait_send)
    lax.fori_loop(1, 16, ctx_send, 0)
    gone(ctx.at[pl.ds(0, 15)], ctx_ss.at[0])

    def turn(sources, landing, base):
        def at_home(cc):
            return jnp.logical_and(y == z, c == cc)

        for cc in range(2):
            copy = remote(
                sources[cc], landing.at[c], tn_ss.at[base, cc], tn_rs.at[base, c], (turned[0], turned[1] + cc)
            )
            pl.when(jnp.logical_not(at_home(cc)))(copy.start)

            @pl.when(at_home(cc))
            def _(cc=cc):
                landing[cc] = sources[cc][...]

            pending.append(lambda cc=cc, copy=copy: pl.when(jnp.logical_not(at_home(cc)))(copy.wait_send))

        def receive():
            for cc in range(2):
                copy = remote(
                    landing.at[cc], landing.at[cc], tn_ss.at[base, cc], tn_rs.at[base, cc], (turned[0], turned[1] + cc)
                )
                pl.when(jnp.logical_not(at_home(cc)))(copy.wait_recv)

        return receive

    res_receive = turn([res_ref.at[pl.ds(cc * 16, 16)] for cc in range(2)], rres, 0)
    ctx[p, :, my_lanes] = ctx_ref[rows_of(c * 16, 16), :]
    ow[:, my_lanes] = ow_ref[...]
    pg[...] = pg_ref[...].reshape(1, WIDTH)
    fg[...] = fg_ref[...].reshape(1, WIDTH)
    for i in range(4):
        block = jnp.broadcast_to(tgt_ref[i : i + 1, :], (128, 128)).T
        for j in range(4):
            for cc in range(2):
                tgt[cc * 256 + (i * 4 + j) * 16 : cc * 256 + (i * 4 + j + 1) * 16, :] = block[
                    j * 32 + cc * 16 : j * 32 + (cc + 1) * 16, :
                ]

    ctx_there = ctx.at[p, :, lanes((1 - c) * 512, 512)]
    landed(ctx_there, sib_rs.at[2])
    ow_there = ow.at[:, lanes((1 - c) * 512, 512)]
    landed(ow_there, sib_rs.at[0])

    group = z * 4 + x
    place16 = lambda g: (y * 4 + g % 4, (g // 4) * 2 + c)

    def attn_copy(g):
        return remote(aout.at[g], ain.at[group], at_ss, at_rs, place16(g))

    for chunk in range(0, 16, CHUNK):
        landed(ctx.at[pl.ds(0, CHUNK - (chunk == 0))], ctx_rs.at[chunk // CHUNK])
        groups = [lax.rem(p + 16 - by, 16) for by in range(chunk, chunk + CHUNK)]
        sums = lax.dot_general(
            jnp.concatenate([ctx[g] for g in groups], axis=0), ow[...], (((1,), (1,)), ((), ())), preferred_element_type=F32
        )
        for i, g in enumerate(groups):
            aout[g] = sums[i * 16 : (i + 1) * 16]
            pl.when(g != group)(attn_copy(g).start)
    gone(aout.at[pl.ds(0, 15)], at_ss)
    ain[group] = aout[group]
    res_receive()
    landed(ain.at[pl.ds(0, 15)], at_rs)
    attn = jnp.concatenate([ain[i] + ain[4 + i] + ain[8 + i] + ain[12 + i] for i in range(4)], axis=1)
    residual = jnp.concatenate([rres[0], rres[1]], axis=1).astype(F32)
    share = lanes(y * SHARE, SHARE)
    post, final = pg[:, share], fg[:, share]

    def y_sum(which, values):
        lane = lax.broadcasted_iota(jnp.int32, (16, 128), 1)
        packed = jnp.zeros((16, 128), F32)
        for i, value in enumerate(values):
            packed = jnp.where(lane == i, jnp.sum(value, axis=1, keepdims=True), packed)
        nbuf[which, y] = packed
        for by in NEAR:
            remote(
                nbuf.at[which, y], nbuf.at[which, y], y_ss.at[which], y_rs.at[which], place(moved(at, "y", by))
            ).start()
        gone(nbuf.at[which, pl.ds(0, 3)], y_ss.at[which])
        landed(nbuf.at[which, pl.ds(0, 3)], y_rs.at[which])
        total = nbuf[which, 0] + nbuf[which, 1] + nbuf[which, 2] + nbuf[which, 3]
        return [total[:, i : i + 1] for i in range(len(values))]

    gained = attn * post
    attn_sq, res_sq, mixed, gained_sq = y_sum(0, [attn * attn, residual * residual, residual * gained, gained * gained])
    inv_attn = lax.rsqrt(attn_sq / WIDTH + epsilon)
    stream = residual + attn * inv_attn * post
    stream_sq = jnp.maximum(res_sq + 2.0 * inv_attn * mixed + inv_attn * inv_attn * gained_sq, 0.0)
    inv_stream = lax.rsqrt(stream_sq / WIDTH + epsilon)
    normed = (stream * inv_stream * final).astype(BF16)
    attn_s[...] = attn
    stream_s[...] = stream
    nbuf[2, 0] = jnp.broadcast_to(inv_attn, (16, 128))
    nbuf[2, 1] = jnp.broadcast_to(inv_stream, (16, 128))

    my_y = lanes(y * 128, 128)
    for q in range(PANELS):
        gath[q, c, z, x, :, my_y] = normed[:, q * 128 : (q + 1) * 128]

    def region(q, here, done):
        return gath.at[
            q,
            here["c"],
            pl.ds(0, 4) if "z" in done else here["z"],
            pl.ds(0, 4) if "x" in done else here["x"],
            :,
            pl.ds(0, 512) if "y" in done else lanes(here["y"] * 128, 128),
        ]

    def ag_start(q, stage):
        dims = GATHER[q % 3]
        src = region(q, at, dims[:stage])
        for by in NEAR:
            remote(src, src, ag_ss.at[stage if stage < 2 else 2 + q // 3], ag_rs.at[q, stage], place(moved(at, dims[stage], by))).start()

    def three_regions(q, stage):
        if stage == 0:
            return gath.at[q, c, 0, pl.ds(0, 3), :, pl.ds(0, 128)]
        if stage == 1:
            return gath.at[q, c, pl.ds(0, 3), :, :, pl.ds(0, 128)]
        return gath.at[q, c, pl.ds(0, 3)]

    def ag_wait(q, stage):
        landed(three_regions(q, stage), ag_rs.at[q, stage])

    for q in range(PANELS):
        ag_start(q, 0)
    for q in range(PANELS):
        ag_wait(q, 0)
        ag_start(q, 1)

    def ag_last(third):
        for q in range(third * 3, third * 3 + 3):
            ag_wait(q, 1)
            ag_start(q, 2)

    def ag_sent(third):
        regions = three_regions(pl.ds(third * 3, 3), 2)
        remote(regions, regions, ag_ss.at[2 + third], ag_ss.at[2 + third], sib).wait_send()

    ag_last(0)
    pltpu.make_async_copy(wv, wv, w_sem).wait()

    def logits(third, which):
        rows = rows_of(which * 256, 256)

        def product(cols):
            total = None
            for q in range(third * 3, third * 3 + 3):
                term = jnp.dot(gath[q, which].reshape(256, 512), wv[q, :, cols], preferred_element_type=F32)
                total = term if total is None else total + term
            return total

        if third == 0:
            for n in range(0, 1024, 512):
                cap[rows, n : n + 512] = product(slice(n, n + 512))
        elif third == 1:
            for n in range(0, 1024, 512):
                cap[rows, n : n + 512] += product(slice(n, n + 512))
        else:
            sums = hits = None
            wanted = tgt[rows, :]
            ids = lax.broadcasted_iota(jnp.int32, (256, 128), 1) + (m * 1024 + p * 8192)
            for n in range(0, 1024, 256):
                total = product(slice(n, n + 256)) + cap[rows, n : n + 256]
                for i in range(0, 256, 128):
                    capped = softcap * jnp.tanh(total[:, i : i + 128] * (1.0 / softcap))
                    cap[rows, n + i : n + i + 128] = capped
                    expd = jnp.exp(capped)
                    hit = jnp.where(ids + (n + i) == wanted, capped, 0.0)
                    sums = expd if sums is None else sums + expd
                    hits = hit if hits is None else hits + hit
            part[rows, :] = sums
            hot[rows, :] = hits

    for stage in range(2):
        gone(three_regions(pl.ds(0, PANELS), stage), ag_ss.at[stage])

    def ag_arrived(third):
        panels = pl.ds(third * 3, 3)
        for q in range(third * 3, third * 3 + 3):
            ag_wait(q, 2)
        remote(gath.at[panels, c], gath.at[panels, c], agc_ss, agc_rs.at[third], sib).start()

    def ag_other(third):
        landed(gath.at[pl.ds(third * 3, 3), 1 - c], agc_rs.at[third])

    ag_sent(0)
    ag_last(1)
    ag_arrived(0)
    logits(0, c)
    ag_sent(1)
    ag_last(2)
    ag_other(0)
    logits(0, 1 - c)
    ag_arrived(1)
    logits(1, c)
    ag_other(1)
    logits(1, 1 - c)
    ag_sent(2)
    ag_arrived(2)
    logits(2, c)
    ag_other(2)
    logits(2, 1 - c)
    gone(gath.at[:, c], agc_ss)

    for i in range(4):
        psrc[i : i + 1, :] = jnp.sum(part[i * 128 : (i + 1) * 128, :].T, axis=0, keepdims=True)
        psrc[i + 4 : i + 5, :] = jnp.sum(hot[i * 128 : (i + 1) * 128, :].T, axis=0, keepdims=True)
    pipe_in[p] = psrc[...]

    def pipe_send(j, _):
        remote(psrc, pipe_in.at[p], tp_ss, tp_rs, (lax.rem(p + j, 16), m)).start()
        return 0

    lax.fori_loop(1, 16, pipe_send, 0)
    gone(pipe_in.at[pl.ds(0, 15)], tp_ss)

    @pl.loop(0, PANELS)
    def _(q):
        turned_q[q] = gath[q].reshape(512, 512).T

    landed(pipe_in.at[pl.ds(0, 15)], tp_rs)
    mp_in[m] = jnp.sum(pipe_in[...], axis=0)

    def mp_send(j, _):
        remote(mp_in.at[m], mp_in.at[m], tm_ss, tm_rs, (p, lax.rem(m + j, 8))).start()
        return 0

    lax.fori_loop(1, 8, mp_send, 0)
    gone(mp_in.at[pl.ds(0, 7)], tm_ss)

    @pl.loop(0, 16)
    def _(block):
        rows = rows_of(block * 32, 32)
        wanted = tgt[rows, :]
        ids = lax.broadcasted_iota(jnp.int32, (32, 128), 1) + (m * 1024 + p * 8192)
        for j in range(8):
            cols = slice(j * 128, (j + 1) * 128)
            capped = cap[rows, cols]
            ratio = capped * (1.0 / softcap)
            slope = 1.0 - ratio * ratio
            cap[rows, cols] = jnp.exp(capped) * slope
            aim[rows, cols] = jnp.where(ids + j * 128 == wanted, slope, 0.0)

    landed(mp_in.at[pl.ds(0, 7)], tm_rs)
    sums = jnp.sum(mp_in[...], axis=0)
    totals, target_logit = sums[:4], sums[4:]
    loss_out[...] = jnp.sum(
        jnp.sum(jnp.log(totals) - target_logit, axis=0, keepdims=True), axis=1, keepdims=True
    ) * (1.0 / 512)
    inverse = 1.0 / totals
    for i in range(4):
        scale[i * 128 : (i + 1) * 128, :] = jnp.broadcast_to(inverse[i : i + 1, :], (128, 128)).T

    def logit_grad(which):
        @pl.loop(0, 4)
        def _(block):
            rows = rows_of(which * 256 + block * 64, 64)
            inv = scale[rows, :]
            for j in range(8):
                cols = slice(j * 128, (j + 1) * 128)
                grad[rows, cols] = (cap[rows, cols] * inv - aim[rows, cols]).astype(BF16)

    def grad_dot(q, which):
        rows = rows_of(which * 256, 256)
        return lax.dot_general(grad[rows, :], wv[q], (((1,), (1,)), ((), ())), preferred_element_type=F32).reshape(
            4, 4, 16, 512
        )

    def rs_sib(q):
        sib_out[q] = grad_dot(q, 1 - c).astype(BF16)
        remote(sib_out.at[q], sib_in.at[q], rc_ss, rc_rs.at[q], sib).start()

    def piece(ref, dim, index, left, lead):
        where = list(lead)
        for d in ("z", "x"):
            if d in left:
                where.append(index if d == dim else pl.ds(0, 4))
        where.append(pl.ds(0, 16))
        if "y" in left:
            where.append(lanes(index * 128, 128) if dim == "y" else pl.ds(0, 512))
        else:
            where.append(pl.ds(0, 128))
        return tuple(where)

    r1 = (r1a, r1b, r1c)
    r2 = (r2a, r2b, r2c)
    dims_of = lambda q: GATHER[q % 3][::-1]

    def rs_first(q):
        landed(sib_in.at[q], rc_rs.at[q])
        first[q] = (keep[q] + sib_in[q].astype(F32)).astype(BF16)
        dim = dims_of(q)[0]
        for by in NEAR:
            there = moved(at, dim, by)
            src = first.at[piece(first, dim, there[dim], ("z", "x", "y"), (q,))]
            remote(src, r1[q % 3].at[q // 3, by - 1], rs_ss.at[q % 3, 0], rs_rs.at[q, 0], place(there)).start()

    def rs_second(q):
        k, r = q % 3, q // 3
        got = r1[k].at[r]
        landed(got, rs_rs.at[q, 0])
        dims = dims_of(q)
        left = [d for d in ("z", "x", "y") if d != dims[0]]
        own = piece(keep, dims[0], at[dims[0]], ("z", "x", "y"), (q,))
        total = keep[own] + sib_in[own].astype(F32)
        total = total + got[0].astype(F32) + got[1].astype(F32) + got[2].astype(F32)
        own2[k][r] = total
        s2[k][r] = total.astype(BF16)
        for by in NEAR:
            there = moved(at, dims[1], by)
            src = s2[k].at[piece(s2[k], dims[1], there[dims[1]], left, (r,))]
            remote(src, r2[k].at[r, by - 1], rs_ss.at[q % 3, 1], rs_rs.at[q, 1], place(there)).start()

    def rs_third(q):
        k, r = q % 3, q // 3
        got = r2[k].at[r]
        landed(got, rs_rs.at[q, 1])
        dims = dims_of(q)
        left = [d for d in ("z", "x", "y") if d != dims[0]]
        total = own2[k][piece(own2[k], dims[1], at[dims[1]], left, (r,))]
        total = total + got[0].astype(F32) + got[1].astype(F32) + got[2].astype(F32)
        s3[k][r] = total
        for by in NEAR:
            there = moved(at, dims[2], by)
            src = s3[k].at[piece(s3[k], dims[2], there[dims[2]], [dims[2]], (r,))]
            remote(src, r3.at[q, by - 1], rs_ss.at[q % 3, 2], rs_rs.at[q, 2], place(there)).start()

    def rs_last(q):
        k, r = q % 3, q // 3
        landed(r3.at[q], rs_rs.at[q, 2])
        dims = dims_of(q)
        own = s3[k][piece(s3[k], dims[2], at[dims[2]], [dims[2]], (r,))]
        gsum[:, q * 128 : (q + 1) * 128] = own + r3[q, 0] + r3[q, 1] + r3[q, 2]

    def head_early(q):
        x_out[q] = jnp.dot(turned_q[q], grad[...], preferred_element_type=F32).astype(BF16).reshape(4, 128, 1024)

    logit_grad(1 - c)
    rs_sib(0)
    logit_grad(c)
    rs_sib(1)
    for q in range(PANELS):
        keep[q] = grad_dot(q, c)
        if q + 2 < PANELS:
            rs_sib(q + 2)
        rs_first(q)
    head_early(0)
    for q in range(PANELS):
        rs_second(q)
    for q in (1, 2, 3):
        head_early(q)
    for q in range(PANELS):
        rs_third(q)
    for q in (4, 5):
        head_early(q)
    for q in range(PANELS):
        rs_last(q)
    gone(sib_out, rc_ss)
    for k in range(3):
        gone(r1[k], rs_ss.at[k, 0])
        gone(r2[k], rs_ss.at[k, 1])
        gone(r3.at[pl.ds(0, 3)], rs_ss.at[k, 2])

    stream, attn = stream_s[...], attn_s[...]
    inv_attn, inv_stream = nbuf[2, 0][:, :1], nbuf[2, 1][:, :1]
    post, final = pg[:, share], fg[:, share]
    upstream = gsum[...] * final
    gained = attn * post
    cross, cross_up, cross_stream = y_sum(1, [stream * upstream, gained * upstream, gained * stream])
    factor = inv_stream * inv_stream * (cross / WIDTH)
    grad_stream = inv_stream * (upstream - stream * factor)
    cross_attn = inv_stream * (cross_up - factor * cross_stream)
    grad_attn = (inv_attn * (grad_stream * post - attn * (inv_attn * inv_attn) * (cross_attn / WIDTH))).astype(BF16)
    for i in range(4):
        gout[i] = grad_attn[:, i * COLS : (i + 1) * COLS]

    def ga_send(j, _):
        g = lax.rem(group + j, 16)
        remote(gout.at[g % 4], gin.at[group], ga_ss, ga_rs, place16(g)).start()
        return 0

    lax.fori_loop(1, 16, ga_send, 0)
    gone(gin.at[pl.ds(0, 15)], ga_ss)
    gin[group] = gout[x]
    d_res = grad_stream.astype(BF16)
    dsend[0] = d_res[:, :576]
    dsend[1] = d_res[:, 576:]
    dres_receive = turn([dsend.at[0], dsend.at[1]], drecv, 1)
    for q in (6, 7):
        head_early(q)
    landed(gin.at[pl.ds(0, 15)], ga_rs)
    ga = gin[...].reshape(256, COLS)
    dcs[...] = jnp.dot(ga, ow[...], preferred_element_type=F32).astype(BF16).reshape(16, 16, 1024)

    def dc_send(j, _):
        i = peer32(j)
        remote(
            dcs.at[i // 2, :, lanes((i % 2) * 512, 512)], dcr.at[me], dc_ss, dc_rs, place32(i)
        ).start()
        return 0

    lax.fori_loop(1, 32, dc_send, 0)
    dcr[me] = dcs[p, :, my_lanes]

    def og_dot(which):
        heads = ctx[:, :, lanes(which * 512, 512)].reshape(256, 512)
        return lax.dot_general(ga, heads, (((0,), (0,)), ((), ())), preferred_element_type=F32)

    ogs[...] = og_dot(1 - c)
    og_copy = remote(ogs, ogr, sib_ss.at[1], sib_rs.at[1], sib)
    og_copy.start()
    og_own = og_dot(c)
    og_copy.wait_recv()
    og_out[...] = (og_own + ogr[...]).astype(BF16)
    head_early(8)
    dres_receive()
    for cc in range(2):
        dres_out[cc * 16 : (cc + 1) * 16, :] = drecv[cc]

    finish()
    og_copy.wait_send()

    landed(dcr.at[pl.ds(0, 31)], dc_rs)
    remote(dcr.at[pl.ds(0, 31)], dcr.at[pl.ds(0, 31)], dc_ss, dc_rs, sib).wait_send()
    for cc in range(2):
        total = dcr[cc].astype(F32)
        for i in range(1, 16):
            total = total + dcr[2 * i + cc].astype(F32)
        dctx_out[cc * 16 : (cc + 1) * 16, :] = total.astype(BF16)


def section_listed(*refs):
    ins, outs, rest = refs[:7], refs[7:12], refs[12:]
    names, n = [], 0
    for count in LAYOUT:
        names.append(rest[n] if count == 1 else tuple(rest[n : n + count]))
        n += count
    section(*ins, *outs, *names)


VM = pltpu.VMEM
DMA = pltpu.SemaphoreType.DMA
SCRATCH = [
    VM((9, 512, 1024), BF16),
    VM((16, 16, 1024), BF16),
    VM((COLS, 1024), BF16),
    VM((1, WIDTH), F32),
    VM((1, WIDTH), F32),
    VM((2, 16, 576), BF16),
    VM((16, 16, COLS), F32),
    VM((16, 16, COLS), F32),
    VM((16, SHARE), F32),
    VM((16, SHARE), F32),
    VM((3, 4, 16, 128), F32),
    VM((9, 2, 4, 4, 16, 512), BF16),
    VM((9, 512, 512), BF16),
    VM((512, 1024), F32),
    VM((512, 128), jnp.int32),
    VM((512, 128), F32),
    VM((512, 128), F32),
    VM((8, 128), F32),
    VM((16, 8, 128), F32),
    VM((8, 8, 128), F32),
    VM((512, 128), F32),
    VM((512, 1024), F32),
    VM((512, 1024), BF16),
    VM((9, 4, 4, 16, 512), F32),
    VM((9, 4, 4, 16, 512), BF16),
    VM((9, 4, 4, 16, 512), BF16),
    VM((9, 4, 4, 16, 512), BF16),
    VM((3, 3, 4, 16, 512), BF16),
    VM((3, 3, 4, 4, 16, 128), BF16),
    VM((3, 3, 4, 16, 512), BF16),
    (VM((3, 4, 16, 512), BF16), VM((3, 4, 4, 16, 128), BF16), VM((3, 4, 16, 512), BF16)),
    (VM((3, 4, 16, 512), F32), VM((3, 4, 4, 16, 128), F32), VM((3, 4, 16, 512), F32)),
    VM((3, 3, 16, 512), BF16),
    VM((3, 3, 4, 16, 128), BF16),
    VM((3, 3, 4, 16, 128), BF16),
    (VM((3, 16, 512), F32), VM((3, 4, 16, 128), F32), VM((3, 4, 16, 128), F32)),
    VM((9, 3, 16, 128), F32),
    VM((16, SHARE), F32),
    VM((4, 16, COLS), BF16),
    VM((16, 16, COLS), BF16),
    VM((16, 16, 1024), BF16),
    VM((32, 16, 512), BF16),
    VM((COLS, 512), F32),
    VM((COLS, 512), F32),
    VM((2, 16, 576), BF16),
    VM((2, 16, 576), BF16),
    DMA,
    DMA((1,)), DMA((16 // CHUNK,)),
    DMA((3,)), DMA((3,)),
    DMA((2, 2)), DMA((2, 2)),
    DMA, DMA,
    DMA((2,)), DMA((2,)),
    DMA((5,)), DMA((9, 3)),
    DMA, DMA((3,)),
    DMA, DMA,
    DMA, DMA,
    DMA, DMA((9,)),
    DMA((3, 3)), DMA((9, 3)),
    DMA, DMA,
    DMA, DMA,
]
LAYOUT = [len(s) if type(s) is tuple else 1 for s in SCRATCH]
FLAT = [t for s in SCRATCH for t in (s if type(s) is tuple else (s,))]


def hand_over_kernel(
    x_any, loss_in, og_in, dres_in, dctx_in, hg_hbm, loss_ref, og_out, dres_out, dctx_out, out_sem, small_sem
):
    outs = [pltpu.make_async_copy(x_any.at[q], hg_hbm.at[:, q], out_sem.at[q]) for q in range(PANELS)]
    small = ((og_in, og_out), (dres_in, dres_out), (dctx_in, dctx_out))
    outs += [pltpu.make_async_copy(a, b, small_sem.at[i]) for i, (a, b) in enumerate(small)]
    for copy in outs:
        copy.start()
    loss_ref[...] = loss_in[...]
    for copy in outs:
        copy.wait()


def on_device(context, residual_in, o_weight, post_gain, final_gain, head_weight, targets):
    vmem, hbm = pl.BlockSpec(memory_space=pltpu.VMEM), pl.BlockSpec(memory_space=pl.ANY)
    shape = jax.ShapeDtypeStruct
    small = [shape((1, 1), F32), shape((COLS, 512), BF16), shape((32, 576), BF16), shape((32, 512), BF16)]
    early, loss, og, dres, dctx = pl.pallas_call(
        section_listed,
        out_shape=[VM(a.shape, a.dtype) for a in (shape((9, 4, 128, 1024), BF16), *small)],
        in_specs=[vmem, vmem, vmem, vmem, vmem, hbm, vmem],
        out_specs=[vmem, vmem, vmem, vmem, vmem],
        scratch_shapes=FLAT,
        compiler_params=pltpu.CompilerParams(
            collective_id=0, has_side_effects=True, vmem_limit_bytes=46 * 2**20
        ),
        cost_estimate=pl.CostEstimate(flops=10**10, bytes_accessed=20 * 10**6, transcendentals=10**6),
        name="section",
    )(
        context,
        residual_in,
        o_weight.T,
        post_gain,
        final_gain,
        head_weight.reshape(4, 9, 128, 1024),
        targets.reshape(4, 128),
    )
    head_grad, loss, og, dres, dctx = pl.pallas_call(
        hand_over_kernel,
        out_shape=[shape((4, 9, 128, 1024), BF16), *small],
        in_specs=[vmem, vmem, vmem, vmem, vmem],
        out_specs=[hbm, vmem, hbm, hbm, hbm],
        scratch_shapes=[DMA((PANELS,)), DMA((3,))],
        compiler_params=pltpu.CompilerParams(vmem_limit_bytes=16 * 2**20),
        cost_estimate=pl.CostEstimate(flops=0, bytes_accessed=20 * 10**6, transcendentals=0),
        name="hand_over",
    )(early, loss, og, dres, dctx)
    return (loss.reshape(()), head_grad.reshape(WIDTH, 1024), og.T, dres, dctx)


def solution(mesh):
    placed = (
        P("pipe", "mp"),
        P("pipe", "mp"),
        P("mp", "pipe"),
        P(),
        P(),
        P(None, ("pipe", "mp")),
        P(),
    )
    return jax.shard_map(
        on_device,
        mesh=mesh,
        in_specs=placed,
        out_specs=(P(), P(None, ("pipe", "mp")), P("mp", "pipe"), P("pipe", "mp"), P("pipe", "mp")),
        check_vma=False,
    )
```

```python
import jax
import jax.numpy as jnp
from jax import lax
from jax.experimental import pallas as pl
from jax.experimental.pallas import tpu as pltpu
from jax.sharding import PartitionSpec as P

epsilon = 1e-06
softcap = 30.0
MESH = pl.DeviceIdType.MESH
F32, BF16 = jnp.float32, jnp.bfloat16

WIDTH = 4608
SHARE = 1152
PANELS = 9
AHEAD = 2
CHUNK = 8
COLS = 288
GATHER = (("y", "x", "z"), ("x", "z", "y"), ("z", "y", "x"))
NEAR = (1, 3, 2)


def remote(src, dst, send, recv, device):
    return pltpu.make_async_remote_copy(
        src_ref=src, dst_ref=dst, send_sem=send, recv_sem=recv, device_id=device, device_id_type=MESH
    )


def place(at):
    return (at["y"] * 4 + at["x"], at["z"] * 2 + at["c"])


def moved(at, dim, by):
    size = 2 if dim == "c" else 4
    return {**at, dim: lax.rem(at[dim] + by, size)}


def lanes(start, size):
    return pl.ds(pl.multiple_of(start, 128), size)


def rows_of(start, size):
    return pl.ds(pl.multiple_of(start, 16), size)


def section(
    ctx_ref, res_ref, ow_ref, pg_ref, fg_ref, w_hbm, tgt_ref,
    x_out, loss_out, og_out, dres_out, dctx_out,
    wv, ctx, ow, pg, fg, rres, aout, ain, attn_s, stream_s, nbuf, gath, turned_q, cap, tgt, hot, part,
    psrc, pipe_in, mp_in, scale, aim, rise16, rises, falls, grad,
    keep, sib_out, sib_in, first, r1a, r1b, r1c, s2, own2, r2a, r2b, r2c, s3, r3, rd,
    gsum, gout, gin, dcs, dcr, ogs, ogr, dsend, drecv,
    w_sem, ctx_ss, ctx_rs, sib_ss, sib_rs, tn_ss, tn_rs, at_ss, at_rs, y_ss, y_rs, ag_ss, ag_rs, agp_ss, agp_rs, agc_ss, agc_rs, tp_ss, tp_rs, tm_ss, tm_rs,
    rc_ss, rc_rs, rs_ss, rs_rs, rsp_ss, rsp_rs, ga_ss, ga_rs, dc_ss, dc_rs,
):
    p, m = lax.axis_index("pipe"), lax.axis_index("mp")
    y, x, z, c = p // 4, p % 4, m // 2, m % 2
    at = {"y": y, "x": x, "z": z, "c": c}
    sib = (p, z * 2 + (1 - c))
    me = p * 2 + c
    peer32 = lambda j: lax.rem(me + j, 32)
    place32 = lambda i: (i // 2, z * 2 + i % 2)

    w_copies = [
        pltpu.make_async_copy(w_hbm.at[i], wv.at[:, pl.ds(i * 128, 128), :], w_sem) for i in range(4)
    ]
    for copy in w_copies:
        copy.start()

    pending = []

    def finish():
        for wait in pending:
            wait()

    def landed(like, sem):
        remote(like, like, sem, sem, sib).wait_recv()

    def gone(like, sem):
        pending.append(remote(like, like, sem, sem, sib).wait_send)

    barrier = pltpu.get_barrier_semaphore()

    def greet(device):
        pl.semaphore_signal(barrier, inc=1, device_id=device, device_id_type=MESH)

    def greet32(j, _):
        greet(place32(peer32(j)))
        return 0

    lax.fori_loop(1, 32, greet32, 0)
    for by in (1, 2, 3):
        zz = lax.rem(z + by, 4)
        greet((p, zz * 2 + (1 - c)))
        for xx in range(4):
            greet((y * 4 + xx, zz * 2 + c))
    turned = (z * 4 + x, y * 2)

    @pl.when(y != z)
    def _():
        for cc in range(2):
            greet((turned[0], turned[1] + cc))

    pl.semaphore_wait(barrier, 46 + 2 * jnp.where(y != z, 1, 0))

    my_lanes = lanes(c * 512, 512)

    def ctx_copy(by, h):
        there = lax.rem(p + by, 16)
        src = ctx_ref.at[rows_of(h * 16, 16)]
        return remote(src, ctx.at[p, :, my_lanes], ctx_ss.at[0], ctx_rs.at[by // CHUNK], (there, z * 2 + h))

    def ctx_send(by, _):
        for h in range(2):
            ctx_copy(by, h).start()
        return 0

    ctx_home = remote(
        ctx_ref.at[rows_of((1 - c) * 16, 16)], ctx.at[p, :, my_lanes], sib_ss.at[2], sib_rs.at[2], sib
    )
    ctx_home.start()
    pending.append(ctx_home.wait_send)
    ow_copy = remote(ow_ref, ow.at[:, my_lanes], sib_ss.at[0], sib_rs.at[0], sib)
    ow_copy.start()
    pending.append(ow_copy.wait_send)
    lax.fori_loop(1, 16, ctx_send, 0)
    gone(ctx.at[pl.ds(0, 15)], ctx_ss.at[0])

    def turn(sources, landing, base):
        def at_home(cc):
            return jnp.logical_and(y == z, c == cc)

        for cc in range(2):
            copy = remote(
                sources[cc], landing.at[c], tn_ss.at[base, cc], tn_rs.at[base, c], (turned[0], turned[1] + cc)
            )
            pl.when(jnp.logical_not(at_home(cc)))(copy.start)

            @pl.when(at_home(cc))
            def _(cc=cc):
                landing[cc] = sources[cc][...]

            pending.append(lambda cc=cc, copy=copy: pl.when(jnp.logical_not(at_home(cc)))(copy.wait_send))

        def receive():
            for cc in range(2):
                copy = remote(
                    landing.at[cc], landing.at[cc], tn_ss.at[base, cc], tn_rs.at[base, cc], (turned[0], turned[1] + cc)
                )
                pl.when(jnp.logical_not(at_home(cc)))(copy.wait_recv)

        return receive

    res_receive = turn([res_ref.at[pl.ds(cc * 16, 16)] for cc in range(2)], rres, 0)
    ctx[p, :, my_lanes] = ctx_ref[rows_of(c * 16, 16), :]
    ow[:, my_lanes] = ow_ref[...]
    pg[...] = pg_ref[...].reshape(1, WIDTH)
    fg[...] = fg_ref[...].reshape(1, WIDTH)
    for i in range(4):
        block = jnp.broadcast_to(tgt_ref[i : i + 1, :], (128, 128)).T
        for j in range(4):
            for cc in range(2):
                tgt[cc * 256 + (i * 4 + j) * 16 : cc * 256 + (i * 4 + j + 1) * 16, :] = block[
                    j * 32 + cc * 16 : j * 32 + (cc + 1) * 16, :
                ]

    ctx_there = ctx.at[p, :, lanes((1 - c) * 512, 512)]
    landed(ctx_there, sib_rs.at[2])
    ow_there = ow.at[:, lanes((1 - c) * 512, 512)]
    landed(ow_there, sib_rs.at[0])

    group = z * 4 + x
    place16 = lambda g: (y * 4 + g % 4, (g // 4) * 2 + c)

    def attn_copy(g):
        return remote(aout.at[g], ain.at[group], at_ss, at_rs, place16(g))

    for chunk in range(0, 16, CHUNK):
        landed(ctx.at[pl.ds(0, CHUNK - (chunk == 0))], ctx_rs.at[chunk // CHUNK])
        groups = [lax.rem(p + 16 - by, 16) for by in range(chunk, chunk + CHUNK)]
        sums = lax.dot_general(
            jnp.concatenate([ctx[g] for g in groups], axis=0), ow[...], (((1,), (1,)), ((), ())), preferred_element_type=F32
        )
        for i, g in enumerate(groups):
            aout[g] = sums[i * 16 : (i + 1) * 16]
            pl.when(g != group)(attn_copy(g).start)
    gone(aout.at[pl.ds(0, 15)], at_ss)
    ain[group] = aout[group]
    res_receive()
    landed(ain.at[pl.ds(0, 15)], at_rs)
    attn = jnp.concatenate([ain[i] + ain[4 + i] + ain[8 + i] + ain[12 + i] for i in range(4)], axis=1)
    residual = jnp.concatenate([rres[0], rres[1]], axis=1).astype(F32)
    share = lanes(y * SHARE, SHARE)
    post, final = pg[:, share], fg[:, share]

    def y_sum(which, values):
        lane = lax.broadcasted_iota(jnp.int32, (16, 128), 1)
        packed = jnp.zeros((16, 128), F32)
        for i, value in enumerate(values):
            packed = jnp.where(lane == i, jnp.sum(value, axis=1, keepdims=True), packed)
        nbuf[which, y] = packed
        for by in NEAR:
            remote(
                nbuf.at[which, y], nbuf.at[which, y], y_ss.at[which], y_rs.at[which], place(moved(at, "y", by))
            ).start()
        gone(nbuf.at[which, pl.ds(0, 3)], y_ss.at[which])
        landed(nbuf.at[which, pl.ds(0, 3)], y_rs.at[which])
        total = nbuf[which, 0] + nbuf[which, 1] + nbuf[which, 2] + nbuf[which, 3]
        return [total[:, i : i + 1] for i in range(len(values))]

    gained = attn * post
    attn_sq, res_sq, mixed, gained_sq = y_sum(0, [attn * attn, residual * residual, residual * gained, gained * gained])
    inv_attn = lax.rsqrt(attn_sq / WIDTH + epsilon)
    stream = residual + attn * inv_attn * post
    stream_sq = jnp.maximum(res_sq + 2.0 * inv_attn * mixed + inv_attn * inv_attn * gained_sq, 0.0)
    inv_stream = lax.rsqrt(stream_sq / WIDTH + epsilon)
    normed = (stream * inv_stream * final).astype(BF16)
    attn_s[...] = attn
    stream_s[...] = stream
    nbuf[2, 0] = jnp.broadcast_to(inv_attn, (16, 128))
    nbuf[2, 1] = jnp.broadcast_to(inv_stream, (16, 128))

    my_y = lanes(y * 128, 128)
    for q in range(PANELS):
        gath[q, c, z, x, :, my_y] = normed[:, q * 128 : (q + 1) * 128]

    def region(q, here, done):
        return gath.at[
            q,
            here["c"],
            pl.ds(0, 4) if "z" in done else here["z"],
            pl.ds(0, 4) if "x" in done else here["x"],
            :,
            pl.ds(0, 512) if "y" in done else lanes(here["y"] * 128, 128),
        ]

    def ag_start(q, stage):
        dims = GATHER[q % 3]
        src = region(q, at, dims[:stage])
        for by in NEAR:
            remote(src, src, ag_ss.at[stage if stage < 2 else 2 + q // 3], ag_rs.at[q, stage], place(moved(at, dims[stage], by))).start()

    def three_regions(q, stage):
        if stage == 0:
            return gath.at[q, c, 0, pl.ds(0, 3), :, pl.ds(0, 128)]
        if stage == 1:
            return gath.at[q, c, pl.ds(0, 3), :, :, pl.ds(0, 128)]
        return gath.at[q, c, pl.ds(0, 3)]

    def ag_wait(q, stage):
        landed(three_regions(q, stage), ag_rs.at[q, stage])

    def planes(j, dims):
        return moved(moved(at, dims[0], j // 4), dims[1], j % 4)

    def ag_plane(j, _):
        for q in range(3):
            src = region(q, at, ())
            remote(src, src, agp_ss, agp_rs.at[q], place(planes(j, GATHER[q]))).start()
        return 0

    lax.fori_loop(1, 16, ag_plane, 0)
    gone(turned_q.at[pl.ds(0, 3), pl.ds(0, 240), pl.ds(0, 128)], agp_ss)
    for q in range(3, PANELS):
        ag_start(q, 0)
    for q in range(3, PANELS):
        ag_wait(q, 0)
        ag_start(q, 1)

    def ag_last(third):
        for q in range(third * 3, third * 3 + 3):
            if third == 0:
                landed(turned_q.at[q, pl.ds(0, 240), pl.ds(0, 128)], agp_rs.at[q])
            else:
                ag_wait(q, 1)
            ag_start(q, 2)

    def ag_sent(third):
        regions = three_regions(pl.ds(third * 3, 3), 2)
        remote(regions, regions, ag_ss.at[2 + third], ag_ss.at[2 + third], sib).wait_send()

    ag_last(0)
    pltpu.make_async_copy(wv, wv, w_sem).wait()

    def logits(third, which):
        rows = rows_of(which * 256, 256)

        def product(cols):
            total = None
            for q in range(third * 3, third * 3 + 3):
                term = jnp.dot(gath[q, which].reshape(256, 512), wv[q, :, cols], preferred_element_type=F32)
                total = term if total is None else total + term
            return total

        if third == 0:
            for n in range(0, 1024, 512):
                cap[rows, n : n + 512] = product(slice(n, n + 512))
        elif third == 1:
            for n in range(0, 1024, 512):
                cap[rows, n : n + 512] += product(slice(n, n + 512))
        else:
            sums = hits = None
            wanted = tgt[rows, :]
            ids = lax.broadcasted_iota(jnp.int32, (256, 128), 1) + (m * 1024 + p * 8192)
            for n in range(0, 1024, 256):
                total = product(slice(n, n + 256)) + cap[rows, n : n + 256]
                for i in range(0, 256, 128):
                    capped = softcap * jnp.tanh(total[:, i : i + 128] * (1.0 / softcap))
                    cap[rows, n + i : n + i + 128] = capped
                    expd = jnp.exp(capped)
                    hit = jnp.where(ids + (n + i) == wanted, capped, 0.0)
                    sums = expd if sums is None else sums + expd
                    hits = hit if hits is None else hits + hit
            part[rows, :] = sums
            hot[rows, :] = hits

    for stage in range(2):
        gone(three_regions(pl.ds(3, PANELS - 3), stage), ag_ss.at[stage])

    def ag_arrived(third):
        panels = pl.ds(third * 3, 3)
        for q in range(third * 3, third * 3 + 3):
            ag_wait(q, 2)
        remote(gath.at[panels, c], gath.at[panels, c], agc_ss, agc_rs.at[third], sib).start()

    def ag_other(third):
        landed(gath.at[pl.ds(third * 3, 3), 1 - c], agc_rs.at[third])

    ag_sent(0)
    ag_last(1)
    ag_arrived(0)
    logits(0, c)
    ag_sent(1)
    ag_last(2)
    ag_other(0)
    logits(0, 1 - c)
    ag_arrived(1)
    logits(1, c)
    ag_other(1)
    logits(1, 1 - c)
    ag_sent(2)
    ag_arrived(2)
    logits(2, c)
    ag_other(2)
    logits(2, 1 - c)
    gone(gath.at[:, c], agc_ss)

    for i in range(4):
        psrc[i : i + 1, :] = jnp.sum(part[i * 128 : (i + 1) * 128, :].T, axis=0, keepdims=True)
        psrc[i + 4 : i + 5, :] = jnp.sum(hot[i * 128 : (i + 1) * 128, :].T, axis=0, keepdims=True)
    pipe_in[p] = psrc[...]

    def pipe_send(j, _):
        remote(psrc, pipe_in.at[p], tp_ss, tp_rs, (lax.rem(p + j, 16), m)).start()
        return 0

    lax.fori_loop(1, 16, pipe_send, 0)
    gone(pipe_in.at[pl.ds(0, 15)], tp_ss)

    @pl.loop(0, 16)
    def _(block):
        rows = rows_of(block * 32, 32)
        wanted = tgt[rows, :]
        ids = lax.broadcasted_iota(jnp.int32, (32, 128), 1) + (m * 1024 + p * 8192)
        for j in range(8):
            cols = slice(j * 128, (j + 1) * 128)
            capped = cap[rows, cols]
            ratio = capped * (1.0 / softcap)
            slope = 1.0 - ratio * ratio
            rise, fall = jnp.exp(capped) * slope, jnp.where(ids + j * 128 == wanted, slope, 0.0)
            cap[rows, cols] = rise
            aim[rows, cols] = fall
            rise16[rows, cols] = rise.astype(BF16)
            grad[rows, cols] = fall.astype(BF16)

    def product_of(terms, q, which):
        rows = rows_of(which * 256, 256)
        return lax.dot_general(terms[rows, :], wv[q], (((1,), (1,)), ((), ())), preferred_element_type=F32)

    def ahead(q):
        for i, which in enumerate((1 - c, c)):
            rises[q, i] = product_of(rise16, q, which)
            falls[q, i] = product_of(grad, q, which)

    ahead(0)
    landed(pipe_in.at[pl.ds(0, 15)], tp_rs)
    mp_in[m] = jnp.sum(pipe_in[...], axis=0)

    def mp_send(j, _):
        remote(mp_in.at[m], mp_in.at[m], tm_ss, tm_rs, (p, lax.rem(m + j, 8))).start()
        return 0

    lax.fori_loop(1, 8, mp_send, 0)
    gone(mp_in.at[pl.ds(0, 7)], tm_ss)

    ahead(1)
    landed(mp_in.at[pl.ds(0, 7)], tm_rs)
    sums = jnp.sum(mp_in[...], axis=0)
    totals, target_logit = sums[:4], sums[4:]
    loss_out[...] = jnp.sum(
        jnp.sum(jnp.log(totals) - target_logit, axis=0, keepdims=True), axis=1, keepdims=True
    ) * (1.0 / 512)
    inverse = 1.0 / totals
    for i in range(4):
        scale[i * 128 : (i + 1) * 128, :] = jnp.broadcast_to(inverse[i : i + 1, :], (128, 128)).T

    def logit_grad(which):
        @pl.loop(0, 4)
        def _(block):
            rows = rows_of(which * 256 + block * 64, 64)
            inv = scale[rows, :]
            for j in range(8):
                cols = slice(j * 128, (j + 1) * 128)
                grad[rows, cols] = (cap[rows, cols] * inv - aim[rows, cols]).astype(BF16)

    def grad_dot(q, which):
        rows = rows_of(which * 256, 256)
        return lax.dot_general(grad[rows, :], wv[q], (((1,), (1,)), ((), ())), preferred_element_type=F32).reshape(
            4, 4, 16, 512
        )

    def rs_sib(q):
        sib_out[q] = (grad_dot(q, 1 - c) if q >= AHEAD else joined(q, 0, 1 - c)).astype(BF16)
        remote(sib_out.at[q], sib_in.at[q], rc_ss, rc_rs.at[q], sib).start()

    def piece(ref, dim, index, left, lead):
        where = list(lead)
        for d in ("z", "x"):
            if d in left:
                where.append(index if d == dim else pl.ds(0, 4))
        where.append(pl.ds(0, 16))
        if "y" in left:
            where.append(lanes(index * 128, 128) if dim == "y" else pl.ds(0, 512))
        else:
            where.append(pl.ds(0, 128))
        return tuple(where)

    r1 = (r1a, r1b, r1c)
    r2 = (r2a, r2b, r2c)
    dims_of = lambda q: GATHER[q % 3][::-1]

    def rs_first(q):
        landed(sib_in.at[q], rc_rs.at[q])
        first[q] = (keep[q] + sib_in[q].astype(F32)).astype(BF16)
        dim = dims_of(q)[0]
        for by in NEAR:
            there = moved(at, dim, by)
            src = first.at[piece(first, dim, there[dim], ("z", "x", "y"), (q,))]
            remote(src, r1[q % 3].at[q // 3, by - 1], rs_ss.at[q % 3, 0], rs_rs.at[q, 0], place(there)).start()

    def rs_block(k, there):
        where = [d for d in ("z", "x") if d != dims_of(k)[0]]
        cols = pl.ds(0, 128) if k == 1 else lanes(there["y"] * 128, 128)
        return (2, *(there[d] for d in where), pl.ds(0, 16), cols)

    def rs_second(q):
        k, r = q % 3, q // 3
        got = r1[k].at[r]
        landed(got, rs_rs.at[q, 0])
        dims = dims_of(q)
        left = [d for d in ("z", "x", "y") if d != dims[0]]
        own = piece(keep, dims[0], at[dims[0]], ("z", "x", "y"), (q,))
        total = keep[own] + sib_in[own].astype(F32)
        total = total + got[0].astype(F32) + got[1].astype(F32) + got[2].astype(F32)
        own2[k][r] = total
        s2[k][r] = total.astype(BF16)
        if r == 2:
            def rs_plane(j, _):
                there = planes(j, dims[1:])
                remote(
                    s2[k].at[rs_block(k, there)], rd.at[k, j], rsp_ss, rsp_rs.at[k], place(there)
                ).start()
                return 0

            lax.fori_loop(1, 16, rs_plane, 0)
            return
        for by in NEAR:
            there = moved(at, dims[1], by)
            src = s2[k].at[piece(s2[k], dims[1], there[dims[1]], left, (r,))]
            remote(src, r2[k].at[r, by - 1], rs_ss.at[q % 3, 1], rs_rs.at[q, 1], place(there)).start()

    def rs_third(q):
        k, r = q % 3, q // 3
        got = r2[k].at[r]
        landed(got, rs_rs.at[q, 1])
        dims = dims_of(q)
        left = [d for d in ("z", "x", "y") if d != dims[0]]
        total = own2[k][piece(own2[k], dims[1], at[dims[1]], left, (r,))]
        total = total + got[0].astype(F32) + got[1].astype(F32) + got[2].astype(F32)
        s3[k][r] = total
        for by in NEAR:
            there = moved(at, dims[2], by)
            src = s3[k].at[piece(s3[k], dims[2], there[dims[2]], [dims[2]], (r,))]
            remote(src, r3.at[q, by - 1], rs_ss.at[q % 3, 2], rs_rs.at[q, 2], place(there)).start()

    def rs_last(q):
        k, r = q % 3, q // 3
        landed(r3.at[q], rs_rs.at[q, 2])
        dims = dims_of(q)
        own = s3[k][piece(s3[k], dims[2], at[dims[2]], [dims[2]], (r,))]
        gsum[:, q * 128 : (q + 1) * 128] = own + r3[q, 0] + r3[q, 1] + r3[q, 2]

    def head_early(q):
        x_out[q] = jnp.dot(turned_q[q], grad[...], preferred_element_type=F32).astype(BF16).reshape(4, 128, 1024)

    def joined(q, i, which):
        inv = scale[rows_of(which * 256, 256), :]
        return jnp.concatenate(
            [rises[q, i, :, n : n + 128] * inv - falls[q, i, :, n : n + 128] for n in range(0, 512, 128)], axis=1
        ).reshape(4, 4, 16, 512)

    rs_sib(0)
    rs_sib(1)
    keep[0] = joined(0, 1, c)
    keep[1] = joined(1, 1, c)
    logit_grad(1 - c)
    logit_grad(c)
    for q in range(PANELS):
        if q >= AHEAD:
            keep[q] = grad_dot(q, c)
        if q + 2 < PANELS:
            rs_sib(q + 2)
        rs_first(q)
    @pl.loop(0, PANELS)
    def _(q):
        turned_q[q] = gath[q].reshape(512, 512).T

    head_early(0)
    for q in range(PANELS):
        rs_second(q)
    for q in (1, 2, 3):
        head_early(q)
    for q in range(PANELS - 3):
        rs_third(q)
    for q in (4, 5):
        head_early(q)
    for q in range(PANELS - 3):
        rs_last(q)
    gone(rd.at[:, pl.ds(1, 15)], rsp_ss)
    for k in range(3):
        landed(rd.at[k, pl.ds(1, 15)], rsp_rs.at[k])
        total = own2[k][rs_block(k, at)]
        for j in range(1, 16):
            total = total + rd[k, j].astype(F32)
        gsum[:, (k + 6) * 128 : (k + 7) * 128] = total
    gone(sib_out, rc_ss)
    for k in range(3):
        gone(r1[k], rs_ss.at[k, 0])
        gone(r2[k].at[pl.ds(0, 2)], rs_ss.at[k, 1])
        gone(r3.at[pl.ds(0, 2)], rs_ss.at[k, 2])

    stream, attn = stream_s[...], attn_s[...]
    inv_attn, inv_stream = nbuf[2, 0][:, :1], nbuf[2, 1][:, :1]
    post, final = pg[:, share], fg[:, share]
    upstream = gsum[...] * final
    gained = attn * post
    cross, cross_up, cross_stream = y_sum(1, [stream * upstream, gained * upstream, gained * stream])
    factor = inv_stream * inv_stream * (cross / WIDTH)
    grad_stream = inv_stream * (upstream - stream * factor)
    cross_attn = inv_stream * (cross_up - factor * cross_stream)
    grad_attn = (inv_attn * (grad_stream * post - attn * (inv_attn * inv_attn) * (cross_attn / WIDTH))).astype(BF16)
    for i in range(4):
        gout[i] = grad_attn[:, i * COLS : (i + 1) * COLS]

    def ga_send(j, _):
        g = lax.rem(group + j, 16)
        remote(gout.at[g % 4], gin.at[group], ga_ss, ga_rs, place16(g)).start()
        return 0

    lax.fori_loop(1, 16, ga_send, 0)
    gone(gin.at[pl.ds(0, 15)], ga_ss)
    gin[group] = gout[x]
    d_res = grad_stream.astype(BF16)
    dsend[0] = d_res[:, :576]
    dsend[1] = d_res[:, 576:]
    dres_receive = turn([dsend.at[0], dsend.at[1]], drecv, 1)
    for q in (6, 7):
        head_early(q)
    landed(gin.at[pl.ds(0, 15)], ga_rs)
    ga = gin[...].reshape(256, COLS)
    dcs[...] = jnp.dot(ga, ow[...], preferred_element_type=F32).astype(BF16).reshape(16, 16, 1024)

    def dc_send(j, _):
        i = peer32(j)
        remote(
            dcs.at[i // 2, :, lanes((i % 2) * 512, 512)], dcr.at[me], dc_ss, dc_rs, place32(i)
        ).start()
        return 0

    lax.fori_loop(1, 32, dc_send, 0)
    dcr[me] = dcs[p, :, my_lanes]

    def og_dot(which):
        heads = ctx[:, :, lanes(which * 512, 512)].reshape(256, 512)
        return lax.dot_general(ga, heads, (((0,), (0,)), ((), ())), preferred_element_type=F32)

    ogs[...] = og_dot(1 - c)
    og_copy = remote(ogs, ogr, sib_ss.at[1], sib_rs.at[1], sib)
    og_copy.start()
    og_own = og_dot(c)
    og_copy.wait_recv()
    og_out[...] = (og_own + ogr[...]).astype(BF16)
    head_early(8)
    dres_receive()
    for cc in range(2):
        dres_out[cc * 16 : (cc + 1) * 16, :] = drecv[cc]

    finish()
    og_copy.wait_send()

    landed(dcr.at[pl.ds(0, 31)], dc_rs)
    remote(dcr.at[pl.ds(0, 31)], dcr.at[pl.ds(0, 31)], dc_ss, dc_rs, sib).wait_send()
    for cc in range(2):
        total = dcr[cc].astype(F32)
        for i in range(1, 16):
            total = total + dcr[2 * i + cc].astype(F32)
        dctx_out[cc * 16 : (cc + 1) * 16, :] = total.astype(BF16)


def section_listed(*refs):
    ins, outs, rest = refs[:7], refs[7:12], refs[12:]
    names, n = [], 0
    for count in LAYOUT:
        names.append(rest[n] if count == 1 else tuple(rest[n : n + count]))
        n += count
    section(*ins, *outs, *names)


VM = pltpu.VMEM
DMA = pltpu.SemaphoreType.DMA
SCRATCH = [
    VM((9, 512, 1024), BF16),
    VM((16, 16, 1024), BF16),
    VM((COLS, 1024), BF16),
    VM((1, WIDTH), F32),
    VM((1, WIDTH), F32),
    VM((2, 16, 576), BF16),
    VM((16, 16, COLS), F32),
    VM((16, 16, COLS), F32),
    VM((16, SHARE), F32),
    VM((16, SHARE), F32),
    VM((3, 4, 16, 128), F32),
    VM((9, 2, 4, 4, 16, 512), BF16),
    VM((9, 512, 512), BF16),
    VM((512, 1024), F32),
    VM((512, 128), jnp.int32),
    VM((512, 128), F32),
    VM((512, 128), F32),
    VM((8, 128), F32),
    VM((16, 8, 128), F32),
    VM((8, 8, 128), F32),
    VM((512, 128), F32),
    VM((512, 1024), F32),
    VM((512, 1024), BF16),
    VM((AHEAD, 2, 256, 512), F32),
    VM((AHEAD, 2, 256, 512), F32),
    VM((512, 1024), BF16),
    VM((9, 4, 4, 16, 512), F32),
    VM((9, 4, 4, 16, 512), BF16),
    VM((9, 4, 4, 16, 512), BF16),
    VM((9, 4, 4, 16, 512), BF16),
    VM((3, 3, 4, 16, 512), BF16),
    VM((3, 3, 4, 4, 16, 128), BF16),
    VM((3, 3, 4, 16, 512), BF16),
    (VM((3, 4, 16, 512), BF16), VM((3, 4, 4, 16, 128), BF16), VM((3, 4, 16, 512), BF16)),
    (VM((3, 4, 16, 512), F32), VM((3, 4, 4, 16, 128), F32), VM((3, 4, 16, 512), F32)),
    VM((3, 3, 16, 512), BF16),
    VM((3, 3, 4, 16, 128), BF16),
    VM((3, 3, 4, 16, 128), BF16),
    (VM((3, 16, 512), F32), VM((3, 4, 16, 128), F32), VM((3, 4, 16, 128), F32)),
    VM((9, 3, 16, 128), F32),
    VM((3, 16, 16, 128), BF16),
    VM((16, SHARE), F32),
    VM((4, 16, COLS), BF16),
    VM((16, 16, COLS), BF16),
    VM((16, 16, 1024), BF16),
    VM((32, 16, 512), BF16),
    VM((COLS, 512), F32),
    VM((COLS, 512), F32),
    VM((2, 16, 576), BF16),
    VM((2, 16, 576), BF16),
    DMA,
    DMA((1,)), DMA((16 // CHUNK,)),
    DMA((3,)), DMA((3,)),
    DMA((2, 2)), DMA((2, 2)),
    DMA, DMA,
    DMA((2,)), DMA((2,)),
    DMA((5,)), DMA((9, 3)),
    DMA, DMA((3,)),
    DMA, DMA((3,)),
    DMA, DMA,
    DMA, DMA,
    DMA, DMA((9,)),
    DMA((3, 3)), DMA((9, 3)),
    DMA, DMA((3,)),
    DMA, DMA,
    DMA, DMA,
]
LAYOUT = [len(s) if type(s) is tuple else 1 for s in SCRATCH]
FLAT = [t for s in SCRATCH for t in (s if type(s) is tuple else (s,))]


def hand_over_kernel(
    x_any, loss_in, og_in, dres_in, dctx_in, hg_hbm, loss_ref, og_out, dres_out, dctx_out, out_sem, small_sem
):
    outs = [pltpu.make_async_copy(x_any.at[q], hg_hbm.at[:, q], out_sem.at[q]) for q in range(PANELS)]
    small = ((og_in, og_out), (dres_in, dres_out), (dctx_in, dctx_out))
    outs += [pltpu.make_async_copy(a, b, small_sem.at[i]) for i, (a, b) in enumerate(small)]
    for copy in outs:
        copy.start()
    loss_ref[...] = loss_in[...]
    for copy in outs:
        copy.wait()


def on_device(context, residual_in, o_weight, post_gain, final_gain, head_weight, targets):
    vmem, hbm = pl.BlockSpec(memory_space=pltpu.VMEM), pl.BlockSpec(memory_space=pl.ANY)
    shape = jax.ShapeDtypeStruct
    small = [shape((1, 1), F32), shape((COLS, 512), BF16), shape((32, 576), BF16), shape((32, 512), BF16)]
    early, loss, og, dres, dctx = pl.pallas_call(
        section_listed,
        out_shape=[VM(a.shape, a.dtype) for a in (shape((9, 4, 128, 1024), BF16), *small)],
        in_specs=[vmem, vmem, vmem, vmem, vmem, hbm, vmem],
        out_specs=[vmem, vmem, vmem, vmem, vmem],
        scratch_shapes=FLAT,
        compiler_params=pltpu.CompilerParams(
            collective_id=0, has_side_effects=True, vmem_limit_bytes=52 * 2**20
        ),
        cost_estimate=pl.CostEstimate(flops=10**10, bytes_accessed=20 * 10**6, transcendentals=10**6),
        name="section",
    )(
        context,
        residual_in,
        o_weight.T,
        post_gain,
        final_gain,
        head_weight.reshape(4, 9, 128, 1024),
        targets.reshape(4, 128),
    )
    head_grad, loss, og, dres, dctx = pl.pallas_call(
        hand_over_kernel,
        out_shape=[shape((4, 9, 128, 1024), BF16), *small],
        in_specs=[vmem, vmem, vmem, vmem, vmem],
        out_specs=[hbm, vmem, hbm, hbm, hbm],
        scratch_shapes=[DMA((PANELS,)), DMA((3,))],
        compiler_params=pltpu.CompilerParams(vmem_limit_bytes=16 * 2**20),
        cost_estimate=pl.CostEstimate(flops=0, bytes_accessed=20 * 10**6, transcendentals=0),
        name="hand_over",
    )(early, loss, og, dres, dctx)
    return (loss.reshape(()), head_grad.reshape(WIDTH, 1024), og.T, dres, dctx)


def solution(mesh):
    placed = (
        P("pipe", "mp"),
        P("pipe", "mp"),
        P("mp", "pipe"),
        P(),
        P(),
        P(None, ("pipe", "mp")),
        P(),
    )
    return jax.shard_map(
        on_device,
        mesh=mesh,
        in_specs=placed,
        out_specs=(P(), P(None, ("pipe", "mp")), P("mp", "pipe"), P("pipe", "mp"), P("pipe", "mp")),
        check_vma=False,
    )
```

```python
import jax
import jax.numpy as jnp
from jax import lax
from jax.experimental import pallas as pl
from jax.experimental.pallas import tpu as pltpu
from jax.sharding import PartitionSpec as P

epsilon = 1e-06
softcap = 30.0
MESH = pl.DeviceIdType.MESH
F32, BF16 = jnp.float32, jnp.bfloat16

WIDTH = 4608
SHARE = 1152
PANELS = 9
AHEAD = 2
CHUNK = 4
COLS = 288
GATHER = (("y", "x", "z"), ("x", "z", "y"), ("z", "y", "x"))
NEAR = (1, 3, 2)


def remote(src, dst, send, recv, device):
    return pltpu.make_async_remote_copy(
        src_ref=src, dst_ref=dst, send_sem=send, recv_sem=recv, device_id=device, device_id_type=MESH
    )


def place(at):
    return (at["y"] * 4 + at["x"], at["z"] * 2 + at["c"])


def moved(at, dim, by):
    size = 2 if dim == "c" else 4
    return {**at, dim: lax.rem(at[dim] + by, size)}


def lanes(start, size):
    return pl.ds(pl.multiple_of(start, 128), size)


def rows_of(start, size):
    return pl.ds(pl.multiple_of(start, 16), size)


def section(
    ctx_ref, res_ref, ow_ref, pg_ref, fg_ref, w_hbm, tgt_ref,
    x_out, loss_out, og_out, dres_out, dctx_out,
    wv, ctx, ow, pg, fg, rres, aout, ain, attn_s, stream_s, nbuf, gath, turned_q, cap, tgt, hot, part,
    psrc, pipe_in, mp_in, scale, aim, rise16, rises, falls, grad,
    keep, sib_out, sib_in, first, r1a, r1b, r1c, s2, own2, r2a, r2b, r2c, s3, r3, rd,
    gsum, gout, gin, dcs, dcr, ogs, ogr, dsend, drecv,
    w_sem, ctx_ss, ctx_rs, sib_ss, sib_rs, tn_ss, tn_rs, at_ss, at_rs, y_ss, y_rs, ag_ss, ag_rs, agp_ss, agp_rs, agc_ss, agc_rs, tp_ss, tp_rs, tm_ss, tm_rs,
    rc_ss, rc_rs, rs_ss, rs_rs, rsp_ss, rsp_rs, ga_ss, ga_rs, dc_ss, dc_rs,
):
    p, m = lax.axis_index("pipe"), lax.axis_index("mp")
    y, x, z, c = p // 4, p % 4, m // 2, m % 2
    at = {"y": y, "x": x, "z": z, "c": c}
    sib = (p, z * 2 + (1 - c))
    me = p * 2 + c
    peer32 = lambda j: lax.rem(me + j, 32)
    place32 = lambda i: (i // 2, z * 2 + i % 2)

    w_copies = [
        pltpu.make_async_copy(w_hbm.at[i], wv.at[:, pl.ds(i * 128, 128), :], w_sem) for i in range(4)
    ]
    for copy in w_copies:
        copy.start()

    pending = []

    def finish():
        for wait in pending:
            wait()

    def landed(like, sem):
        remote(like, like, sem, sem, sib).wait_recv()

    def gone(like, sem):
        pending.append(remote(like, like, sem, sem, sib).wait_send)

    barrier = pltpu.get_barrier_semaphore()

    def greet(device):
        pl.semaphore_signal(barrier, inc=1, device_id=device, device_id_type=MESH)

    def greet32(j, _):
        greet(place32(peer32(j)))
        return 0

    lax.fori_loop(1, 32, greet32, 0)
    for by in (1, 2, 3):
        zz = lax.rem(z + by, 4)
        greet((p, zz * 2 + (1 - c)))
        for xx in range(4):
            greet((y * 4 + xx, zz * 2 + c))
    turned = (z * 4 + x, y * 2)

    @pl.when(y != z)
    def _():
        for cc in range(2):
            greet((turned[0], turned[1] + cc))

    pl.semaphore_wait(barrier, 46 + 2 * jnp.where(y != z, 1, 0))

    my_lanes = lanes(c * 512, 512)

    def ctx_copy(by, h):
        there = lax.rem(p + by, 16)
        src = ctx_ref.at[rows_of(h * 16, 16)]
        return remote(src, ctx.at[p, :, my_lanes], ctx_ss.at[0], ctx_rs.at[by // CHUNK], (there, z * 2 + h))

    def ctx_send(by, _):
        for h in range(2):
            ctx_copy(by, h).start()
        return 0

    ctx_home = remote(
        ctx_ref.at[rows_of((1 - c) * 16, 16)], ctx.at[p, :, my_lanes], sib_ss.at[2], sib_rs.at[2], sib
    )
    ctx_home.start()
    pending.append(ctx_home.wait_send)
    ow_copy = remote(ow_ref, ow.at[:, my_lanes], sib_ss.at[0], sib_rs.at[0], sib)
    ow_copy.start()
    pending.append(ow_copy.wait_send)
    lax.fori_loop(1, 16, ctx_send, 0)
    gone(ctx.at[pl.ds(0, 15)], ctx_ss.at[0])

    def turn(sources, landing, base):
        def at_home(cc):
            return jnp.logical_and(y == z, c == cc)

        for cc in range(2):
            copy = remote(
                sources[cc], landing.at[c], tn_ss.at[base, cc], tn_rs.at[base, c], (turned[0], turned[1] + cc)
            )
            pl.when(jnp.logical_not(at_home(cc)))(copy.start)

            @pl.when(at_home(cc))
            def _(cc=cc):
                landing[cc] = sources[cc][...]

            pending.append(lambda cc=cc, copy=copy: pl.when(jnp.logical_not(at_home(cc)))(copy.wait_send))

        def receive():
            for cc in range(2):
                copy = remote(
                    landing.at[cc], landing.at[cc], tn_ss.at[base, cc], tn_rs.at[base, cc], (turned[0], turned[1] + cc)
                )
                pl.when(jnp.logical_not(at_home(cc)))(copy.wait_recv)

        return receive

    res_receive = turn([res_ref.at[pl.ds(cc * 16, 16)] for cc in range(2)], rres, 0)
    ctx[p, :, my_lanes] = ctx_ref[rows_of(c * 16, 16), :]
    ow[:, my_lanes] = ow_ref[...]
    pg[...] = pg_ref[...].reshape(1, WIDTH)
    fg[...] = fg_ref[...].reshape(1, WIDTH)
    for i in range(4):
        block = jnp.broadcast_to(tgt_ref[i : i + 1, :], (128, 128)).T
        for j in range(4):
            for cc in range(2):
                tgt[cc * 256 + (i * 4 + j) * 16 : cc * 256 + (i * 4 + j + 1) * 16, :] = block[
                    j * 32 + cc * 16 : j * 32 + (cc + 1) * 16, :
                ]

    ctx_there = ctx.at[p, :, lanes((1 - c) * 512, 512)]
    landed(ctx_there, sib_rs.at[2])
    ow_there = ow.at[:, lanes((1 - c) * 512, 512)]
    landed(ow_there, sib_rs.at[0])

    group = z * 4 + x
    place16 = lambda g: (y * 4 + g % 4, (g // 4) * 2 + c)

    def attn_copy(g):
        return remote(aout.at[g], ain.at[group], at_ss, at_rs, place16(g))

    for chunk in range(0, 16, CHUNK):
        landed(ctx.at[pl.ds(0, CHUNK - (chunk == 0))], ctx_rs.at[chunk // CHUNK])
        groups = [lax.rem(p + 16 - by, 16) for by in range(chunk, chunk + CHUNK)]
        sums = lax.dot_general(
            jnp.concatenate([ctx[g] for g in groups], axis=0), ow[...], (((1,), (1,)), ((), ())), preferred_element_type=F32
        )
        for i, g in enumerate(groups):
            aout[g] = sums[i * 16 : (i + 1) * 16]
            pl.when(g != group)(attn_copy(g).start)
    gone(aout.at[pl.ds(0, 15)], at_ss)
    ain[group] = aout[group]
    res_receive()
    landed(ain.at[pl.ds(0, 15)], at_rs)
    attn = jnp.concatenate([ain[i] + ain[4 + i] + ain[8 + i] + ain[12 + i] for i in range(4)], axis=1)
    residual = jnp.concatenate([rres[0], rres[1]], axis=1).astype(F32)
    share = lanes(y * SHARE, SHARE)
    post, final = pg[:, share], fg[:, share]

    def y_sum(which, values):
        lane = lax.broadcasted_iota(jnp.int32, (16, 128), 1)
        packed = jnp.zeros((16, 128), F32)
        for i, value in enumerate(values):
            packed = jnp.where(lane == i, jnp.sum(value, axis=1, keepdims=True), packed)
        nbuf[which, y] = packed
        for by in NEAR:
            remote(
                nbuf.at[which, y], nbuf.at[which, y], y_ss.at[which], y_rs.at[which], place(moved(at, "y", by))
            ).start()
        gone(nbuf.at[which, pl.ds(0, 3)], y_ss.at[which])
        landed(nbuf.at[which, pl.ds(0, 3)], y_rs.at[which])
        total = nbuf[which, 0] + nbuf[which, 1] + nbuf[which, 2] + nbuf[which, 3]
        return [total[:, i : i + 1] for i in range(len(values))]

    gained = attn * post
    attn_sq, res_sq, mixed, gained_sq = y_sum(0, [attn * attn, residual * residual, residual * gained, gained * gained])
    inv_attn = lax.rsqrt(attn_sq / WIDTH + epsilon)
    stream = residual + attn * inv_attn * post
    stream_sq = jnp.maximum(res_sq + 2.0 * inv_attn * mixed + inv_attn * inv_attn * gained_sq, 0.0)
    inv_stream = lax.rsqrt(stream_sq / WIDTH + epsilon)
    normed = (stream * inv_stream * final).astype(BF16)
    attn_s[...] = attn
    stream_s[...] = stream
    nbuf[2, 0] = jnp.broadcast_to(inv_attn, (16, 128))
    nbuf[2, 1] = jnp.broadcast_to(inv_stream, (16, 128))

    my_y = lanes(y * 128, 128)
    for q in range(PANELS):
        gath[q, c, z, x, :, my_y] = normed[:, q * 128 : (q + 1) * 128]

    def region(q, here, done):
        return gath.at[
            q,
            here["c"],
            pl.ds(0, 4) if "z" in done else here["z"],
            pl.ds(0, 4) if "x" in done else here["x"],
            :,
            pl.ds(0, 512) if "y" in done else lanes(here["y"] * 128, 128),
        ]

    def ag_start(q, stage):
        dims = GATHER[q % 3]
        src = region(q, at, dims[:stage])
        for by in NEAR:
            remote(src, src, ag_ss.at[stage if stage < 2 else 2 + q // 3], ag_rs.at[q, stage], place(moved(at, dims[stage], by))).start()

    def three_regions(q, stage):
        if stage == 0:
            return gath.at[q, c, 0, pl.ds(0, 3), :, pl.ds(0, 128)]
        if stage == 1:
            return gath.at[q, c, pl.ds(0, 3), :, :, pl.ds(0, 128)]
        return gath.at[q, c, pl.ds(0, 3)]

    def ag_wait(q, stage):
        landed(three_regions(q, stage), ag_rs.at[q, stage])

    def planes(j, dims):
        return moved(moved(at, dims[0], j // 4), dims[1], j % 4)

    def ag_plane(j, _):
        for q in range(3):
            src = region(q, at, ())
            remote(src, src, agp_ss, agp_rs.at[q], place(planes(j, GATHER[q]))).start()
        return 0

    lax.fori_loop(1, 16, ag_plane, 0)
    gone(turned_q.at[pl.ds(0, 3), pl.ds(0, 240), pl.ds(0, 128)], agp_ss)
    for q in range(3, PANELS):
        ag_start(q, 0)
    for q in range(3, PANELS):
        ag_wait(q, 0)
        ag_start(q, 1)

    def ag_last(third):
        for q in range(third * 3, third * 3 + 3):
            if third == 0:
                landed(turned_q.at[q, pl.ds(0, 240), pl.ds(0, 128)], agp_rs.at[q])
            else:
                ag_wait(q, 1)
            ag_start(q, 2)

    def ag_sent(third):
        regions = three_regions(pl.ds(third * 3, 3), 2)
        remote(regions, regions, ag_ss.at[2 + third], ag_ss.at[2 + third], sib).wait_send()

    ag_last(0)
    pltpu.make_async_copy(wv, wv, w_sem).wait()

    def logits(third, which):
        rows = rows_of(which * 256, 256)

        def product(cols):
            total = None
            for q in range(third * 3, third * 3 + 3):
                term = jnp.dot(gath[q, which].reshape(256, 512), wv[q, :, cols], preferred_element_type=F32)
                total = term if total is None else total + term
            return total

        if third == 0:
            for n in range(0, 1024, 512):
                cap[rows, n : n + 512] = product(slice(n, n + 512))
        elif third == 1:
            for n in range(0, 1024, 512):
                cap[rows, n : n + 512] += product(slice(n, n + 512))
        else:
            sums = hits = None
            wanted = tgt[rows, :]
            ids = lax.broadcasted_iota(jnp.int32, (256, 128), 1) + (m * 1024 + p * 8192)
            for n in range(0, 1024, 256):
                total = product(slice(n, n + 256)) + cap[rows, n : n + 256]
                for i in range(0, 256, 128):
                    capped = softcap * jnp.tanh(total[:, i : i + 128] * (1.0 / softcap))
                    cap[rows, n + i : n + i + 128] = capped
                    expd = jnp.exp(capped)
                    hit = jnp.where(ids + (n + i) == wanted, capped, 0.0)
                    sums = expd if sums is None else sums + expd
                    hits = hit if hits is None else hits + hit
            part[rows, :] = sums
            hot[rows, :] = hits

    for stage in range(2):
        gone(three_regions(pl.ds(3, PANELS - 3), stage), ag_ss.at[stage])

    def ag_arrived(third):
        panels = pl.ds(third * 3, 3)
        for q in range(third * 3, third * 3 + 3):
            ag_wait(q, 2)
        remote(gath.at[panels, c], gath.at[panels, c], agc_ss, agc_rs.at[third], sib).start()

    def ag_other(third):
        landed(gath.at[pl.ds(third * 3, 3), 1 - c], agc_rs.at[third])

    ag_sent(0)
    ag_last(1)
    ag_arrived(0)
    logits(0, c)
    ag_sent(1)
    ag_last(2)
    ag_other(0)
    logits(0, 1 - c)
    ag_arrived(1)
    logits(1, c)
    ag_other(1)
    logits(1, 1 - c)
    ag_sent(2)
    ag_arrived(2)
    logits(2, c)
    ag_other(2)
    logits(2, 1 - c)
    gone(gath.at[:, c], agc_ss)

    for i in range(4):
        psrc[i : i + 1, :] = jnp.sum(part[i * 128 : (i + 1) * 128, :].T, axis=0, keepdims=True)
        psrc[i + 4 : i + 5, :] = jnp.sum(hot[i * 128 : (i + 1) * 128, :].T, axis=0, keepdims=True)
    pipe_in[p] = psrc[...]

    def pipe_send(j, _):
        remote(psrc, pipe_in.at[p], tp_ss, tp_rs, (lax.rem(p + j, 16), m)).start()
        return 0

    lax.fori_loop(1, 16, pipe_send, 0)
    gone(pipe_in.at[pl.ds(0, 15)], tp_ss)

    @pl.loop(0, 16)
    def _(block):
        rows = rows_of(block * 32, 32)
        wanted = tgt[rows, :]
        ids = lax.broadcasted_iota(jnp.int32, (32, 128), 1) + (m * 1024 + p * 8192)
        for j in range(8):
            cols = slice(j * 128, (j + 1) * 128)
            capped = cap[rows, cols]
            ratio = capped * (1.0 / softcap)
            slope = 1.0 - ratio * ratio
            rise, fall = jnp.exp(capped) * slope, jnp.where(ids + j * 128 == wanted, slope, 0.0)
            cap[rows, cols] = rise
            aim[rows, cols] = fall
            rise16[rows, cols] = rise.astype(BF16)
            grad[rows, cols] = fall.astype(BF16)

    def product_of(terms, q, which):
        rows = rows_of(which * 256, 256)
        return lax.dot_general(terms[rows, :], wv[q], (((1,), (1,)), ((), ())), preferred_element_type=F32)

    def ahead(q):
        for i, which in enumerate((1 - c, c)):
            rises[q, i] = product_of(rise16, q, which)
            falls[q, i] = product_of(grad, q, which)

    ahead(0)
    landed(pipe_in.at[pl.ds(0, 15)], tp_rs)
    mp_in[m] = jnp.sum(pipe_in[...], axis=0)

    def mp_send(j, _):
        remote(mp_in.at[m], mp_in.at[m], tm_ss, tm_rs, (p, lax.rem(m + j, 8))).start()
        return 0

    lax.fori_loop(1, 8, mp_send, 0)
    gone(mp_in.at[pl.ds(0, 7)], tm_ss)

    ahead(1)
    landed(mp_in.at[pl.ds(0, 7)], tm_rs)
    sums = jnp.sum(mp_in[...], axis=0)
    totals, target_logit = sums[:4], sums[4:]
    loss_out[...] = jnp.sum(
        jnp.sum(jnp.log(totals) - target_logit, axis=0, keepdims=True), axis=1, keepdims=True
    ) * (1.0 / 512)
    inverse = 1.0 / totals
    for i in range(4):
        scale[i * 128 : (i + 1) * 128, :] = jnp.broadcast_to(inverse[i : i + 1, :], (128, 128)).T

    def logit_grad(which):
        @pl.loop(0, 4)
        def _(block):
            rows = rows_of(which * 256 + block * 64, 64)
            inv = scale[rows, :]
            for j in range(8):
                cols = slice(j * 128, (j + 1) * 128)
                grad[rows, cols] = (cap[rows, cols] * inv - aim[rows, cols]).astype(BF16)

    def grad_dot(q, which):
        rows = rows_of(which * 256, 256)
        return lax.dot_general(grad[rows, :], wv[q], (((1,), (1,)), ((), ())), preferred_element_type=F32).reshape(
            4, 4, 16, 512
        )

    def rs_sib(q):
        sib_out[q] = (grad_dot(q, 1 - c) if q >= AHEAD else joined(q, 0, 1 - c)).astype(BF16)
        remote(sib_out.at[q], sib_in.at[q], rc_ss, rc_rs.at[q], sib).start()

    def piece(ref, dim, index, left, lead):
        where = list(lead)
        for d in ("z", "x"):
            if d in left:
                where.append(index if d == dim else pl.ds(0, 4))
        where.append(pl.ds(0, 16))
        if "y" in left:
            where.append(lanes(index * 128, 128) if dim == "y" else pl.ds(0, 512))
        else:
            where.append(pl.ds(0, 128))
        return tuple(where)

    r1 = (r1a, r1b, r1c)
    r2 = (r2a, r2b, r2c)
    dims_of = lambda q: GATHER[q % 3][::-1]

    def rs_first(q):
        landed(sib_in.at[q], rc_rs.at[q])
        first[q] = (keep[q] + sib_in[q].astype(F32)).astype(BF16)
        dim = dims_of(q)[0]
        for by in NEAR:
            there = moved(at, dim, by)
            src = first.at[piece(first, dim, there[dim], ("z", "x", "y"), (q,))]
            remote(src, r1[q % 3].at[q // 3, by - 1], rs_ss.at[q % 3, 0], rs_rs.at[q, 0], place(there)).start()

    def rs_block(k, there):
        where = [d for d in ("z", "x") if d != dims_of(k)[0]]
        cols = pl.ds(0, 128) if k == 1 else lanes(there["y"] * 128, 128)
        return (2, *(there[d] for d in where), pl.ds(0, 16), cols)

    def rs_second(q):
        k, r = q % 3, q // 3
        got = r1[k].at[r]
        landed(got, rs_rs.at[q, 0])
        dims = dims_of(q)
        left = [d for d in ("z", "x", "y") if d != dims[0]]
        own = piece(keep, dims[0], at[dims[0]], ("z", "x", "y"), (q,))
        total = keep[own] + sib_in[own].astype(F32)
        total = total + got[0].astype(F32) + got[1].astype(F32) + got[2].astype(F32)
        own2[k][r] = total
        s2[k][r] = total.astype(BF16)
        if r == 2:
            def rs_plane(j, _):
                there = planes(j, dims[1:])
                remote(
                    s2[k].at[rs_block(k, there)], rd.at[k, j], rsp_ss, rsp_rs.at[k], place(there)
                ).start()
                return 0

            lax.fori_loop(1, 16, rs_plane, 0)
            return
        for by in NEAR:
            there = moved(at, dims[1], by)
            src = s2[k].at[piece(s2[k], dims[1], there[dims[1]], left, (r,))]
            remote(src, r2[k].at[r, by - 1], rs_ss.at[q % 3, 1], rs_rs.at[q, 1], place(there)).start()

    def rs_third(q):
        k, r = q % 3, q // 3
        got = r2[k].at[r]
        landed(got, rs_rs.at[q, 1])
        dims = dims_of(q)
        left = [d for d in ("z", "x", "y") if d != dims[0]]
        total = own2[k][piece(own2[k], dims[1], at[dims[1]], left, (r,))]
        total = total + got[0].astype(F32) + got[1].astype(F32) + got[2].astype(F32)
        s3[k][r] = total
        for by in NEAR:
            there = moved(at, dims[2], by)
            src = s3[k].at[piece(s3[k], dims[2], there[dims[2]], [dims[2]], (r,))]
            remote(src, r3.at[q, by - 1], rs_ss.at[q % 3, 2], rs_rs.at[q, 2], place(there)).start()

    def rs_last(q):
        k, r = q % 3, q // 3
        landed(r3.at[q], rs_rs.at[q, 2])
        dims = dims_of(q)
        own = s3[k][piece(s3[k], dims[2], at[dims[2]], [dims[2]], (r,))]
        gsum[:, q * 128 : (q + 1) * 128] = own + r3[q, 0] + r3[q, 1] + r3[q, 2]

    def head_early(q):
        x_out[q] = jnp.dot(turned_q[q], grad[...], preferred_element_type=F32).astype(BF16).reshape(4, 128, 1024)

    def joined(q, i, which):
        inv = scale[rows_of(which * 256, 256), :]
        return jnp.concatenate(
            [rises[q, i, :, n : n + 128] * inv - falls[q, i, :, n : n + 128] for n in range(0, 512, 128)], axis=1
        ).reshape(4, 4, 16, 512)

    rs_sib(0)
    rs_sib(1)
    keep[0] = joined(0, 1, c)
    keep[1] = joined(1, 1, c)
    logit_grad(1 - c)
    logit_grad(c)
    for q in range(PANELS):
        if q >= AHEAD:
            keep[q] = grad_dot(q, c)
        if q + 2 < PANELS:
            rs_sib(q + 2)
        rs_first(q)
    @pl.loop(0, PANELS)
    def _(q):
        turned_q[q] = gath[q].reshape(512, 512).T

    head_early(0)
    for q in range(PANELS):
        rs_second(q)
    for q in (1, 2, 3):
        head_early(q)
    for q in range(PANELS - 3):
        rs_third(q)
    for q in (4, 5):
        head_early(q)
    for q in range(PANELS - 3):
        rs_last(q)
    gone(rd.at[:, pl.ds(1, 15)], rsp_ss)
    for k in range(3):
        landed(rd.at[k, pl.ds(1, 15)], rsp_rs.at[k])
        total = own2[k][rs_block(k, at)]
        for j in range(1, 16):
            total = total + rd[k, j].astype(F32)
        gsum[:, (k + 6) * 128 : (k + 7) * 128] = total
    gone(sib_out, rc_ss)
    for k in range(3):
        gone(r1[k], rs_ss.at[k, 0])
        gone(r2[k].at[pl.ds(0, 2)], rs_ss.at[k, 1])
        gone(r3.at[pl.ds(0, 2)], rs_ss.at[k, 2])

    stream, attn = stream_s[...], attn_s[...]
    inv_attn, inv_stream = nbuf[2, 0][:, :1], nbuf[2, 1][:, :1]
    post, final = pg[:, share], fg[:, share]
    upstream = gsum[...] * final
    gained = attn * post
    cross, cross_up, cross_stream = y_sum(1, [stream * upstream, gained * upstream, gained * stream])
    factor = inv_stream * inv_stream * (cross / WIDTH)
    grad_stream = inv_stream * (upstream - stream * factor)
    cross_attn = inv_stream * (cross_up - factor * cross_stream)
    grad_attn = (inv_attn * (grad_stream * post - attn * (inv_attn * inv_attn) * (cross_attn / WIDTH))).astype(BF16)
    for i in range(4):
        gout[i] = grad_attn[:, i * COLS : (i + 1) * COLS]

    def ga_send(j, _):
        g = lax.rem(group + j, 16)
        remote(gout.at[g % 4], gin.at[group], ga_ss, ga_rs, place16(g)).start()
        return 0

    lax.fori_loop(1, 16, ga_send, 0)
    gone(gin.at[pl.ds(0, 15)], ga_ss)
    gin[group] = gout[x]
    d_res = grad_stream.astype(BF16)
    dsend[0] = d_res[:, :576]
    dsend[1] = d_res[:, 576:]
    dres_receive = turn([dsend.at[0], dsend.at[1]], drecv, 1)
    for q in (6, 7):
        head_early(q)
    landed(gin.at[pl.ds(0, 15)], ga_rs)
    ga = gin[...].reshape(256, COLS)
    dcs[...] = jnp.dot(ga, ow[...], preferred_element_type=F32).astype(BF16).reshape(16, 16, 1024)

    def dc_send(j, _):
        i = peer32(j)
        remote(
            dcs.at[i // 2, :, lanes((i % 2) * 512, 512)], dcr.at[me], dc_ss, dc_rs, place32(i)
        ).start()
        return 0

    lax.fori_loop(1, 32, dc_send, 0)
    dcr[me] = dcs[p, :, my_lanes]

    def og_dot(which):
        heads = ctx[:, :, lanes(which * 512, 512)].reshape(256, 512)
        return lax.dot_general(ga, heads, (((0,), (0,)), ((), ())), preferred_element_type=F32)

    ogs[...] = og_dot(1 - c)
    og_copy = remote(ogs, ogr, sib_ss.at[1], sib_rs.at[1], sib)
    og_copy.start()
    og_own = og_dot(c)
    og_copy.wait_recv()
    og_out[...] = (og_own + ogr[...]).astype(BF16)
    head_early(8)
    dres_receive()
    for cc in range(2):
        dres_out[cc * 16 : (cc + 1) * 16, :] = drecv[cc]

    finish()
    og_copy.wait_send()

    landed(dcr.at[pl.ds(0, 31)], dc_rs)
    remote(dcr.at[pl.ds(0, 31)], dcr.at[pl.ds(0, 31)], dc_ss, dc_rs, sib).wait_send()
    for cc in range(2):
        total = dcr[cc].astype(F32)
        for i in range(1, 16):
            total = total + dcr[2 * i + cc].astype(F32)
        dctx_out[cc * 16 : (cc + 1) * 16, :] = total.astype(BF16)


def section_listed(*refs):
    ins, outs, rest = refs[:7], refs[7:12], refs[12:]
    names, n = [], 0
    for count in LAYOUT:
        names.append(rest[n] if count == 1 else tuple(rest[n : n + count]))
        n += count
    section(*ins, *outs, *names)


VM = pltpu.VMEM
DMA = pltpu.SemaphoreType.DMA
SCRATCH = [
    VM((9, 512, 1024), BF16),
    VM((16, 16, 1024), BF16),
    VM((COLS, 1024), BF16),
    VM((1, WIDTH), F32),
    VM((1, WIDTH), F32),
    VM((2, 16, 576), BF16),
    VM((16, 16, COLS), F32),
    VM((16, 16, COLS), F32),
    VM((16, SHARE), F32),
    VM((16, SHARE), F32),
    VM((3, 4, 16, 128), F32),
    VM((9, 2, 4, 4, 16, 512), BF16),
    VM((9, 512, 512), BF16),
    VM((512, 1024), F32),
    VM((512, 128), jnp.int32),
    VM((512, 128), F32),
    VM((512, 128), F32),
    VM((8, 128), F32),
    VM((16, 8, 128), F32),
    VM((8, 8, 128), F32),
    VM((512, 128), F32),
    VM((512, 1024), F32),
    VM((512, 1024), BF16),
    VM((AHEAD, 2, 256, 512), F32),
    VM((AHEAD, 2, 256, 512), F32),
    VM((512, 1024), BF16),
    VM((9, 4, 4, 16, 512), F32),
    VM((9, 4, 4, 16, 512), BF16),
    VM((9, 4, 4, 16, 512), BF16),
    VM((9, 4, 4, 16, 512), BF16),
    VM((3, 3, 4, 16, 512), BF16),
    VM((3, 3, 4, 4, 16, 128), BF16),
    VM((3, 3, 4, 16, 512), BF16),
    (VM((3, 4, 16, 512), BF16), VM((3, 4, 4, 16, 128), BF16), VM((3, 4, 16, 512), BF16)),
    (VM((3, 4, 16, 512), F32), VM((3, 4, 4, 16, 128), F32), VM((3, 4, 16, 512), F32)),
    VM((3, 3, 16, 512), BF16),
    VM((3, 3, 4, 16, 128), BF16),
    VM((3, 3, 4, 16, 128), BF16),
    (VM((3, 16, 512), F32), VM((3, 4, 16, 128), F32), VM((3, 4, 16, 128), F32)),
    VM((9, 3, 16, 128), F32),
    VM((3, 16, 16, 128), BF16),
    VM((16, SHARE), F32),
    VM((4, 16, COLS), BF16),
    VM((16, 16, COLS), BF16),
    VM((16, 16, 1024), BF16),
    VM((32, 16, 512), BF16),
    VM((COLS, 512), F32),
    VM((COLS, 512), F32),
    VM((2, 16, 576), BF16),
    VM((2, 16, 576), BF16),
    DMA,
    DMA((1,)), DMA((16 // CHUNK,)),
    DMA((3,)), DMA((3,)),
    DMA((2, 2)), DMA((2, 2)),
    DMA, DMA,
    DMA((2,)), DMA((2,)),
    DMA((5,)), DMA((9, 3)),
    DMA, DMA((3,)),
    DMA, DMA((3,)),
    DMA, DMA,
    DMA, DMA,
    DMA, DMA((9,)),
    DMA((3, 3)), DMA((9, 3)),
    DMA, DMA((3,)),
    DMA, DMA,
    DMA, DMA,
]
LAYOUT = [len(s) if type(s) is tuple else 1 for s in SCRATCH]
FLAT = [t for s in SCRATCH for t in (s if type(s) is tuple else (s,))]


def hand_over_kernel(
    x_any, loss_in, og_in, dres_in, dctx_in, hg_hbm, loss_ref, og_out, dres_out, dctx_out, out_sem, small_sem
):
    outs = [pltpu.make_async_copy(x_any.at[q], hg_hbm.at[:, q], out_sem.at[q]) for q in range(PANELS)]
    small = ((og_in, og_out), (dres_in, dres_out), (dctx_in, dctx_out))
    outs += [pltpu.make_async_copy(a, b, small_sem.at[i]) for i, (a, b) in enumerate(small)]
    for copy in outs:
        copy.start()
    loss_ref[...] = loss_in[...]
    for copy in outs:
        copy.wait()


def on_device(context, residual_in, o_weight, post_gain, final_gain, head_weight, targets):
    vmem, hbm = pl.BlockSpec(memory_space=pltpu.VMEM), pl.BlockSpec(memory_space=pl.ANY)
    shape = jax.ShapeDtypeStruct
    small = [shape((1, 1), F32), shape((COLS, 512), BF16), shape((32, 576), BF16), shape((32, 512), BF16)]
    early, loss, og, dres, dctx = pl.pallas_call(
        section_listed,
        out_shape=[VM(a.shape, a.dtype) for a in (shape((9, 4, 128, 1024), BF16), *small)],
        in_specs=[vmem, vmem, vmem, vmem, vmem, hbm, vmem],
        out_specs=[vmem, vmem, vmem, vmem, vmem],
        scratch_shapes=FLAT,
        compiler_params=pltpu.CompilerParams(
            collective_id=0, has_side_effects=True, vmem_limit_bytes=52 * 2**20
        ),
        cost_estimate=pl.CostEstimate(flops=10**10, bytes_accessed=20 * 10**6, transcendentals=10**6),
        name="section",
    )(
        context,
        residual_in,
        o_weight.T,
        post_gain,
        final_gain,
        head_weight.reshape(4, 9, 128, 1024),
        targets.reshape(4, 128),
    )
    head_grad, loss, og, dres, dctx = pl.pallas_call(
        hand_over_kernel,
        out_shape=[shape((4, 9, 128, 1024), BF16), *small],
        in_specs=[vmem, vmem, vmem, vmem, vmem],
        out_specs=[hbm, vmem, hbm, hbm, hbm],
        scratch_shapes=[DMA((PANELS,)), DMA((3,))],
        compiler_params=pltpu.CompilerParams(vmem_limit_bytes=16 * 2**20),
        cost_estimate=pl.CostEstimate(flops=0, bytes_accessed=20 * 10**6, transcendentals=0),
        name="hand_over",
    )(early, loss, og, dres, dctx)
    return (loss.reshape(()), head_grad.reshape(WIDTH, 1024), og.T, dres, dctx)


def solution(mesh):
    placed = (
        P("pipe", "mp"),
        P("pipe", "mp"),
        P("mp", "pipe"),
        P(),
        P(),
        P(None, ("pipe", "mp")),
        P(),
    )
    return jax.shard_map(
        on_device,
        mesh=mesh,
        in_specs=placed,
        out_specs=(P(), P(None, ("pipe", "mp")), P("mp", "pipe"), P("pipe", "mp"), P("pipe", "mp")),
        check_vma=False,
    )
```
